256 devices in a mesh: ga: 32 (over z_lo, x, core), band: 8 (over z_hi, y).
Axes of the slice: x: 4, y: 4, z: 8 (z_hi: 2, z_lo: 4; z = z_hi * 4 + z_lo), core: 2. Of those that a mesh axis runs over, the one named last changes fastest.
Arguments:
- trial_block: bfloat16 [512, 2, 32768], P('band', None, 'ga'), may hold values from -6 to 6
- applied_block: bfloat16 [512, 2, 32768], P('band', None, 'ga'), may hold values from -6 to 6
- margin_extra: bfloat16 [512, 2, 32768], P('band', None, 'ga'), may hold values from -1.1953125 to 1.1953125
Outputs:
- rotated_trial: bfloat16 [512, 2, 32768], P('band', None, 'ga')
- rotated_applied: bfloat16 [512, 2, 32768], P('band', None, 'ga')
- rotated_margin: bfloat16 [512, 2, 32768], P('band', None, 'ga')
The draws below stay inside these ranges and needn't reach their ends.
All inputs are finite; a program needn't handle non-finite values.
Results may differ from the reference program's by a relative error of at most 0.006.
Values may be sent and summed in bfloat16 or wider, within the bound.
A program may use at most 128 MiB of HBM per device.

```python
import jax
import jax.numpy as jnp
from jax import lax

M = 512
NG = 32768


def levels(stream_key, shape, cuts, least, top_value):
    level, own = 1.0, jax.random.fold_in(stream_key, 6)
    for axis_at, parts in cuts:
        steps = jnp.exp(jax.random.uniform(jax.random.fold_in(own, axis_at), (parts,), jnp.float32, least / len(cuts), top_value / len(cuts)))
        level = level * jnp.repeat(steps, shape[axis_at] // parts).reshape([-1 if axis == axis_at else 1 for axis in range(len(shape))])
    return level


def scatter_about(rng, shape, spread, bound, split=(), kind=jnp.bfloat16):
    drawn = jax.random.normal(rng, shape, jnp.float32) * spread
    if len(split) > 0:
        drawn = levels(rng, shape, split, -0.22, 0.18) * drawn
    return jnp.clip(drawn, min=-bound, max=bound).astype(kind)


def setup_inputs(seed: int = 0) -> dict:
    keys = jax.random.split(jax.random.key(seed), 4)
    return {
        "trial_block": scatter_about(keys[0], (M, 2, NG), 1.0, 6.0, ((0, 8), (2, 32))),
        "applied_block": scatter_about(keys[1], (M, 2, NG), 1.0, 6.0, ((0, 8), (2, 32))),
        "margin_extra": scatter_about(keys[2], (M, 2, NG), 0.2, 1.1953125, ((0, 8), (2, 32))),
    }


def gram_terms(left, right):
    product = jnp.einsum('icg,jdg->cdij', left.astype(jnp.float32), right.astype(jnp.float32), precision=lax.Precision.HIGHEST)
    return (product[0, 0] + product[1, 1], product[0, 1] - product[1, 0])

def embedding(real_part, imag_part):
    top = jnp.concatenate([real_part, -imag_part], axis=1)
    bottom = jnp.concatenate([imag_part, real_part], axis=1)
    return jnp.concatenate([top, bottom], axis=0)

def rotate(source, rot_real, rot_imag):
    source_f = source.astype(jnp.float32)
    with_real = jnp.einsum('icg,ij->jcg', source_f, rot_real.astype(jnp.float32), precision=lax.Precision.HIGHEST)
    with_imag = jnp.einsum('icg,ij->jcg', source_f, rot_imag.astype(jnp.float32), precision=lax.Precision.HIGHEST)
    return jnp.stack([with_real[:, 0] - with_imag[:, 1], with_real[:, 1] + with_imag[:, 0]], axis=1).astype(jnp.bfloat16)

def reference(trial_block, applied_block, margin_extra):
    margin_block = (trial_block.astype(jnp.float32) + margin_extra.astype(jnp.float32)).astype(jnp.bfloat16)
    ham_real, ham_imag = gram_terms(trial_block, applied_block)
    ovl_real, ovl_imag = gram_terms(trial_block, margin_block)
    ham_real, ham_imag, ovl_real, ovl_imag = (ham_real / NG, ham_imag / NG, ovl_real / NG, ovl_imag / NG)
    hamilt = embedding((ham_real + ham_real.T) * 0.5, (ham_imag - ham_imag.T) * 0.5)
    margin = embedding((ovl_real + ovl_real.T) * 0.5, (ovl_imag - ovl_imag.T) * 0.5)
    factor = jnp.linalg.cholesky(margin)
    half_done = jax.scipy.linalg.solve_triangular(factor, hamilt, lower=True)
    reduced = jax.scipy.linalg.solve_triangular(factor, half_done.T, lower=True).T
    spread_scale = jnp.sqrt(jnp.sum(reduced * reduced) / (2 * M) + 1e-06)
    identity = jnp.eye(2 * M, dtype=jnp.float32)
    shaped = jax.scipy.linalg.solve_triangular(factor, identity - reduced / (2.0 * spread_scale), lower=True, trans=1)
    rotation = jnp.dot(shaped, shaped.T, precision=lax.Precision.HIGHEST).astype(jnp.bfloat16)
    rot_real = rotation[:M, :M]
    rot_imag = rotation[M:, :M]
    return (rotate(trial_block, rot_real, rot_imag), rotate(applied_block, rot_real, rot_imag), rotate(margin_block, rot_real, rot_imag))
```

```python
import functools

import jax
import jax.numpy as jnp
from jax import lax
from jax.experimental import pallas as pl
from jax.experimental.pallas import tpu as pltpu
from jax.sharding import PartitionSpec as P

MESH = pl.DeviceIdType.MESH
F32 = jnp.float32
BF16 = jnp.bfloat16


def iota(shape, dim):
    return lax.broadcasted_iota(jnp.int32, shape, dim)


def remote(src, dst, send_sem, recv_sem, device):
    return pltpu.make_async_remote_copy(
        src_ref=src,
        dst_ref=dst,
        send_sem=send_sem,
        recv_sem=recv_sem,
        device_id=device,
        device_id_type=MESH,
    )


def exchange_kernel(scale, t_ref, x_ref, gt_ref, gx_ref, full_ref, gt, part, core_in, mid, x_in, low, z_in, full,
                    t_send, t_recv, x_send, x_recv, s_send, s_recv, local_sem):
    g = lax.axis_index("ga")
    b = lax.axis_index("band")
    zl, x, c = g // 8, (g // 2) % 4, g % 2
    h, y = b // 4, b % 4
    partner = (1 - h) * 4 + y
    y_up, y_dn, y_far = (y + 1) % 4, (y + 3) % 4, (y + 2) % 4

    def band_at(hh, yy):
        return hh * 4 + yy

    def ga_at(zz, xx, cc):
        return zz * 8 + xx * 2 + cc

    barrier = pltpu.get_barrier_semaphore()
    greet = [(g, (b + d) % 8) for d in range(1, 8)]
    greet += [(ga_at(zl, x, 1 - c), b)]
    greet += [(ga_at(zl, (x + d) % 4, c), b) for d in range(1, 4)]
    greet += [(ga_at((zl + d) % 4, x, c), b) for d in range(1, 4)]
    for device in greet:
        pl.semaphore_signal(barrier, inc=1, device_id=device, device_id_type=MESH)
    pl.semaphore_wait(barrier, len(greet))

    up, dn, over = (g, band_at(h, y_up)), (g, band_at(h, y_dn)), (g, partner)

    def gather(own, slots, half, send, recv):
        def move(n, src, block, rows, device):
            return remote(src, slots.at[block, rows], send.at[n], recv.at[n], device)

        whole = pl.ds(0, 2 * half)
        lo, hi = pl.ds(0, half), pl.ds(half, half)
        b_dn, b_up = band_at(h, y_dn), band_at(h, y_up)
        p_dn, p_up = band_at(1 - h, y_dn), band_at(1 - h, y_up)
        first = [move(0, own, b, whole, over), move(1, own, b, whole, up), move(2, own, b, whole, dn)]
        second = [
            move(3, slots.at[partner], partner, whole, up),
            move(4, slots.at[partner], partner, whole, dn),
            move(5, slots.at[b_dn, lo], b_dn, lo, up),
            move(6, slots.at[b_up, hi], b_up, hi, dn),
            move(7, slots.at[p_dn, lo], p_dn, lo, up),
            move(8, slots.at[p_up, hi], p_up, hi, dn),
        ]

        def start():
            for copy in first:
                copy.start()

        def forward_own():
            first[1].wait_recv()
            second[2].start()
            first[2].wait_recv()
            second[3].start()

        def forward_partner():
            first[0].wait_recv()
            second[0].start()
            second[1].start()

        def forward_far():
            second[0].wait_recv()
            second[4].start()
            second[1].wait_recv()
            second[5].start()

        def finish():
            for copy in second[2:]:
                copy.wait_recv()

        def drain():
            for copy in first + second:
                copy.wait_send()

        return start, forward_own, forward_partner, forward_far, finish, drain

    t_start, t_own, t_partner, t_far, t_finish, t_drain = gather(t_ref, gt, 64, t_send, t_recv)
    x_start, x_own, x_partner, x_far, x_finish, x_drain = gather(x_ref, gx_ref, 128, x_send, x_recv)
    t_start()
    own_t = pltpu.make_async_copy(t_ref, gt.at[b], local_sem.at[0])
    own_t.start()
    own_x = pltpu.make_async_copy(x_ref, gx_ref.at[b], local_sem.at[1])
    own_x.start()
    own_t.wait()
    own_x.wait()
    t_own()
    t_partner()
    t_far()
    t_finish()
    t_drain()
    x_start()

    sign = jnp.where(iota((64, 128), 1) < 64, scale, -scale).astype(F32)

    def gram(k, carry):
        u = lax.dot_general(
            x_ref[...], gt[k], (((1,), (1,)), ((), ())), preferred_element_type=F32
        )
        part[1, k] = u[0:64] * sign + pltpu.roll(u[64:128], 64, 1) * scale
        part[0, k] = u[128:192] * sign + pltpu.roll(u[192:256], 64, 1) * scale
        return carry

    lax.fori_loop(0, 8, gram, 0)

    sib = (ga_at(zl, x, 1 - c), b)
    move = remote(part.at[:, pl.ds((1 - c) * 4, 4)], core_in, s_send.at[0], s_recv.at[0], sib)
    move.start()
    move.wait()
    mid[...] = part[:, pl.ds(c * 4, 4)] + core_in[...]

    moves = [
        remote(mid.at[:, (x + d) % 4], x_in.at[d - 1], s_send.at[d], s_recv.at[d], (ga_at(zl, (x + d) % 4, c), b))
        for d in range(1, 4)
    ]
    for move in moves:
        move.start()
    for move in moves:
        move.wait()
    low[...] = mid[:, x] + x_in[0] + x_in[1] + x_in[2]

    moves = [
        remote(
            low.at[:, pl.ds(((zl + d) % 4) * 16, 16)],
            z_in.at[d - 1],
            s_send.at[3 + d],
            s_recv.at[3 + d],
            (ga_at((zl + d) % 4, x, c), b),
        )
        for d in range(1, 4)
    ]
    for move in moves:
        move.start()
    for move in moves:
        move.wait()
    blk = c * 4 + x
    full[:, blk, b, zl] = low[:, pl.ds(zl * 16, 16)] + z_in[0] + z_in[1] + z_in[2]

    x_own()
    x_partner()

    def spread(view, base, devices):
        moves = [
            remote(view, view, s_send.at[base + n], s_recv.at[base + n], device) for n, device in enumerate(devices)
        ]
        for move in moves:
            move.start()
        for move in moves:
            move.wait()

    spread(full.at[:, blk, b, zl], 7, [(g, (b + d) % 8) for d in range(1, 8)])
    spread(full.at[:, blk, :, zl], 14, [(ga_at((zl + d) % 4, x, c), b) for d in range(1, 4)])
    spread(full.at[:, blk], 17, [(ga_at(zl, (x + d) % 4, c), b) for d in range(1, 4)])
    spread(full.at[:, pl.ds(c * 4, 4)], 20, [sib])

    out_t = pltpu.make_async_copy(gt, gt_ref, local_sem.at[0])
    out_f = pltpu.make_async_copy(full, full_ref, local_sem.at[1])
    out_t.start()
    out_f.start()
    x_far()
    x_finish()
    x_drain()
    out_t.wait()
    out_f.wait()


def exchange(trial, rest, scale):
    vmem = pl.BlockSpec(memory_space=pltpu.VMEM)
    anywhere = pl.BlockSpec(memory_space=pl.ANY)
    sem = pltpu.SemaphoreType.DMA
    return pl.pallas_call(
        functools.partial(exchange_kernel, scale),
        out_shape=(
            jax.ShapeDtypeStruct((8, 128, 1024), BF16),
            jax.ShapeDtypeStruct((8, 256, 1024), BF16),
            jax.ShapeDtypeStruct((2, 8, 8, 4, 16, 128), F32),
        ),
        in_specs=[vmem, vmem],
        out_specs=(anywhere, anywhere, anywhere),
        scratch_shapes=[
            pltpu.VMEM((8, 128, 1024), BF16),
            pltpu.VMEM((2, 8, 64, 128), F32),
            pltpu.VMEM((2, 4, 64, 128), F32),
            pltpu.VMEM((2, 4, 64, 128), F32),
            pltpu.VMEM((3, 2, 64, 128), F32),
            pltpu.VMEM((2, 64, 128), F32),
            pltpu.VMEM((3, 2, 16, 128), F32),
            pltpu.VMEM((2, 8, 8, 4, 16, 128), F32),
            sem((9,)),
            sem((9,)),
            sem((9,)),
            sem((9,)),
            sem((21,)),
            sem((21,)),
            sem((2,)),
        ],
        compiler_params=pltpu.CompilerParams(
            collective_id=0, has_side_effects=True, vmem_limit_bytes=48 * 2**20
        ),
    )(trial, rest)


def invert_pivot(block):
    lane, row = iota((64, 128), 1), iota((64, 128), 0)
    one = lane[:1]
    for k in range(0, 64, 2):
        m = k + 1
        c0r = jnp.broadcast_to(block[:, k : k + 1], (64, 128))
        c0i = jnp.broadcast_to(block[:, 64 + k : 65 + k], (64, 128))
        c1r = jnp.broadcast_to(block[:, m : m + 1], (64, 128))
        c1i = jnp.broadcast_to(block[:, 64 + m : 65 + m], (64, 128))
        r0, r1 = block[k : k + 1, :], block[m : m + 1, :]
        s0, s1 = pltpu.roll(r0, 64, 1), pltpu.roll(r1, 64, 1)
        s0, s1 = jnp.where(one < 64, -s0, s0), jnp.where(one < 64, -s1, s1)
        a, br, bi, c = c0r[k : k + 1], c1r[k : k + 1], c1i[k : k + 1], c1r[m : m + 1]
        e0, e0i, e1, e1i = one == k, one == 64 + k, one == m, one == 64 + m
        r0 = jnp.where(e0, 1.0, jnp.where(e0i | e1 | e1i, 0.0, r0))
        s0 = jnp.where(e0i, 1.0, jnp.where(e0 | e1 | e1i, 0.0, s0))
        r1 = jnp.where(e1, 1.0, jnp.where(e1i | e0 | e0i, 0.0, r1))
        s1 = jnp.where(e1i, 1.0, jnp.where(e1 | e0 | e0i, 0.0, s1))
        ra = 1.0 / a
        tr, ti = br * ra, bi * ra
        rs = 1.0 / (c - (br * br + bi * bi) * ra)
        i01r, i01i = -tr * rs, -ti * rs
        i00 = ra + (tr * tr + ti * ti) * rs
        q0 = i00 * r0 + i01r * r1 + i01i * s1
        q1 = i01r * r0 - i01i * s0 + rs * r1
        u0 = i00 * s0 + i01r * s1 - i01i * r1
        u1 = i01r * s0 + i01i * r0 + rs * s1
        isk, ism = row == k, row == m
        c0r = jnp.where(isk, -1.0, jnp.where(ism, 0.0, c0r))
        c1r = jnp.where(ism, -1.0, jnp.where(isk, 0.0, c1r))
        c0i, c1i = jnp.where(isk | ism, 0.0, c0i), jnp.where(isk | ism, 0.0, c1i)
        dead = isk | ism | (lane == k) | (lane == m) | (lane == 64 + k) | (lane == 64 + m)
        block = jnp.where(dead, 0.0, block) - c0r * q0 - c0i * u0 - c1r * q1 - c1i * u1
    return block


def halves(value):
    high = value.astype(BF16)
    return high, (value - high.astype(F32)).astype(BF16)


def dot(a, b):
    return jnp.dot(a, b, preferred_element_type=F32)


def dot_split(a, b):
    ah, al = halves(a)
    bh, bl = halves(b)
    return dot(ah, bh) + dot(al, bh) + dot(ah, bl)


def times_i(value):
    tiles = [pltpu.roll(value[:, n : n + 128], 64, 1) for n in range(0, value.shape[1], 128)]
    turned = jnp.concatenate(tiles, axis=1)
    return jnp.where(iota(value.shape, 1) % 128 < 64, -turned, turned)


def invert(work):
    def step(k, carry):
        rows, lanes = pl.ds(pl.multiple_of(k * 64, 64), 64), pl.ds(pl.multiple_of(k * 128, 128), 128)
        pivot = invert_pivot(work[rows, lanes])
        panel = work[rows, :]
        panel = dot_split(pivot, jnp.concatenate([panel, times_i(panel)], axis=0))
        panel = jnp.where(iota((64, 1024), 1) // 128 == k, jnp.concatenate([pivot] * 8, axis=1), panel)
        column = jnp.where(iota((512, 128), 0) // 64 == k, 0.0, work[:, lanes])
        work[:, lanes] = jnp.zeros((512, 128), F32)
        work[...] = work[...] - dot_split(column, jnp.concatenate([panel, times_i(panel)], axis=0))
        work[rows, :] = panel
        return carry

    lax.fori_loop(0, 8, step, 0)


def hermitian_part(full, m, out):
    lane = iota((64, 128), 1) < 64

    def row_block(k, carry):
        rows = pl.ds(pl.multiple_of(k * 64, 64), 64)
        for n in range(0, 8, 2):
            turned = full[m, k, pl.ds(64 * n, 128), :].T
            re, im = turned[0:64], -turned[64:128]
            left = jnp.where(lane, re, pltpu.roll(im, 64, 1))
            right = jnp.where(lane, pltpu.roll(re, 64, 1), im)
            out[rows, pl.ds(128 * n, 128)] = (full[m, n, rows, :] + left) * 0.5
            out[rows, pl.ds(128 * n + 128, 128)] = (full[m, n + 1, rows, :] + right) * 0.5
        return carry

    lax.fori_loop(0, 8, row_block, 0)


def expand(value_ref, high, low):
    def row_block(k, carry):
        rows = pl.ds(pl.multiple_of(k * 64, 64), 64)
        value = value_ref[rows, :]
        vh, vl = halves(value)
        th, tl = halves(times_i(value))
        top, bottom = pl.ds(pl.multiple_of(k * 128, 128), 64), pl.ds(pl.multiple_of(k * 128 + 64, 64), 64)
        high[top, :], high[bottom, :], low[top, :], low[bottom, :] = vh, th, vl, tl
        return carry

    lax.fori_loop(0, 8, row_block, 0)


def product(left_ref, rows, high, low, out):
    def column_block(n, carry):
        lanes = pl.ds(pl.multiple_of(n * 256, 256), 256)
        ah, al = halves(left_ref[rows, :])
        bh = high[:, lanes]
        out[:, lanes] = dot(ah, bh) + dot(al, bh) + dot(ah, low[:, lanes])
        return carry

    lax.fori_loop(0, 4, column_block, 0)


def rotate_kernel(full, gt, gx, o_ref, w, ham, p, q, pq, high, low):
    b = lax.axis_index("band")
    own = pl.ds(pl.multiple_of(b * 64, 64), 64)
    hermitian_part(full, 0, w)
    hermitian_part(full, 1, ham)
    invert(w)
    expand(ham, high, low)
    product(w, pl.ds(0, 512), high, low, p)
    expand(w, high, low)
    product(p, pl.ds(0, 512), high, low, q)
    total = jnp.sum(q[...] * ham[...], keepdims=True)
    rs = lax.rsqrt(jnp.maximum(total, 0.0) * (1.0 / 512) + 1e-6)
    expand(q, high, low)
    product(p, own, high, low, pq)
    z = w[own, :] - q[own, :] * rs + pq[...] * (0.25 * rs * rs)
    z = z.astype(BF16).astype(F32)
    turned = times_i(z)
    re_part = jnp.where(iota((64, 1024), 1) % 128 < 64, z, -z)
    im_part = jnp.where(iota((64, 1024), 1) % 128 < 64, -turned, turned)
    weights = jnp.concatenate([re_part, im_part], axis=0).astype(BF16)
    o_ref[0] = dot(weights, gt[...].reshape(1024, 1024)).astype(BF16)
    o_ref[1] = dot(weights, gx[:, 0:128, :].reshape(1024, 1024)).astype(BF16)
    o_ref[2] = dot(weights, gx[:, 128:256, :].reshape(1024, 1024)).astype(BF16)


def rotate(full, gt, gx):
    vmem = pl.BlockSpec(memory_space=pltpu.VMEM)
    return pl.pallas_call(
        rotate_kernel,
        out_shape=jax.ShapeDtypeStruct((3, 128, 1024), BF16),
        in_specs=[vmem] * 3,
        out_specs=vmem,
        scratch_shapes=[
            pltpu.VMEM((512, 1024), F32),
            pltpu.VMEM((512, 1024), F32),
            pltpu.VMEM((512, 1024), F32),
            pltpu.VMEM((512, 1024), F32),
            pltpu.VMEM((64, 1024), F32),
            pltpu.VMEM((1024, 1024), BF16),
            pltpu.VMEM((1024, 1024), BF16),
        ],
        compiler_params=pltpu.CompilerParams(vmem_limit_bytes=48 * 2**20),
    )(full, gt, gx)


def local(trial, applied, extra):
    margin = (trial.astype(F32) + extra.astype(F32)).astype(BF16)
    rows, _, length = trial.shape

    def planes(block):
        return jnp.swapaxes(block, 0, 1).reshape(2 * rows, length)

    rest = jnp.concatenate([planes(applied), planes(margin)], axis=0)
    scale = 1.0 / (length * lax.axis_size("ga"))
    gt, gx, full = exchange(planes(trial), rest, scale)
    out = rotate(full.reshape(2, 8, 512, 128), gt, gx)
    out = out.reshape(3, 2, rows, length)
    return tuple(jnp.swapaxes(out[n], 0, 1) for n in range(3))


def solution(mesh):
    spec = P("band", None, "ga")
    return jax.shard_map(local, mesh=mesh, in_specs=(spec,) * 3, out_specs=(spec,) * 3, check_vma=False)
```

```python
import functools

import jax
import jax.numpy as jnp
from jax import lax
from jax.experimental import pallas as pl
from jax.experimental.pallas import tpu as pltpu
from jax.sharding import PartitionSpec as P

MESH = pl.DeviceIdType.MESH
F32 = jnp.float32
BF16 = jnp.bfloat16


def iota(shape, dim):
    return lax.broadcasted_iota(jnp.int32, shape, dim)


def remote(src, dst, send_sem, recv_sem, device):
    return pltpu.make_async_remote_copy(
        src_ref=src,
        dst_ref=dst,
        send_sem=send_sem,
        recv_sem=recv_sem,
        device_id=device,
        device_id_type=MESH,
    )


def exchange_kernel(scale, t_ref, x_ref, gt_ref, gx_ref, full_ref, gt, part, core_in, mid, x_in, low, z_in, full,
                    t_send, t_recv, x_send, x_recv, s_send, s_recv, local_sem):
    g = lax.axis_index("ga")
    b = lax.axis_index("band")
    zl, x, c = g // 8, (g // 2) % 4, g % 2
    h, y = b // 4, b % 4
    partner = (1 - h) * 4 + y
    y_up, y_dn, y_far = (y + 1) % 4, (y + 3) % 4, (y + 2) % 4

    def band_at(hh, yy):
        return hh * 4 + yy

    def ga_at(zz, xx, cc):
        return zz * 8 + xx * 2 + cc

    barrier = pltpu.get_barrier_semaphore()
    greet = [(g, (b + d) % 8) for d in range(1, 8)]
    greet += [(ga_at(zl, x, 1 - c), b)]
    greet += [(ga_at(zl, (x + d) % 4, c), b) for d in range(1, 4)]
    greet += [(ga_at((zl + d) % 4, x, c), b) for d in range(1, 4)]
    for device in greet:
        pl.semaphore_signal(barrier, inc=1, device_id=device, device_id_type=MESH)
    pl.semaphore_wait(barrier, len(greet))

    up, dn, over = (g, band_at(h, y_up)), (g, band_at(h, y_dn)), (g, partner)

    def gather(own, slots, half, send, recv):
        def move(n, src, block, rows, device):
            return remote(src, slots.at[block, rows], send.at[n], recv.at[n], device)

        whole = pl.ds(0, 2 * half)
        lo, hi = pl.ds(0, half), pl.ds(half, half)
        b_dn, b_up = band_at(h, y_dn), band_at(h, y_up)
        p_dn, p_up = band_at(1 - h, y_dn), band_at(1 - h, y_up)
        first = [move(0, own, b, whole, over), move(1, own, b, whole, up), move(2, own, b, whole, dn)]
        second = [
            move(3, slots.at[partner], partner, whole, up),
            move(4, slots.at[partner], partner, whole, dn),
            move(5, slots.at[b_dn, lo], b_dn, lo, up),
            move(6, slots.at[b_up, hi], b_up, hi, dn),
            move(7, slots.at[p_dn, lo], p_dn, lo, up),
            move(8, slots.at[p_up, hi], p_up, hi, dn),
        ]

        def start():
            for copy in first:
                copy.start()

        def forward_own():
            first[1].wait_recv()
            second[2].start()
            first[2].wait_recv()
            second[3].start()

        def forward_partner():
            first[0].wait_recv()
            second[0].start()
            second[1].start()

        def forward_far():
            second[0].wait_recv()
            second[4].start()
            second[1].wait_recv()
            second[5].start()

        def finish():
            for copy in second[2:]:
                copy.wait_recv()

        def drain():
            for copy in first + second:
                copy.wait_send()

        return start, forward_own, forward_partner, forward_far, finish, drain

    t_start, t_own, t_partner, t_far, t_finish, t_drain = gather(t_ref, gt, 64, t_send, t_recv)
    x_start, x_own, x_partner, x_far, x_finish, x_drain = gather(x_ref, gx_ref, 128, x_send, x_recv)
    t_start()
    own_t = pltpu.make_async_copy(t_ref, gt.at[b], local_sem.at[0])
    own_t.start()
    own_x = pltpu.make_async_copy(x_ref, gx_ref.at[b], local_sem.at[1])
    own_x.start()
    own_t.wait()
    own_x.wait()
    t_own()
    t_partner()
    t_far()
    t_finish()
    t_drain()
    x_start()

    sign = jnp.where(iota((64, 128), 1) < 64, scale, -scale).astype(F32)

    def gram(k, carry):
        u = lax.dot_general(
            x_ref[...], gt[k], (((1,), (1,)), ((), ())), preferred_element_type=F32
        )
        part[1, k] = u[0:64] * sign + pltpu.roll(u[64:128], 64, 1) * scale
        part[0, k] = u[128:192] * sign + pltpu.roll(u[192:256], 64, 1) * scale
        return carry

    lax.fori_loop(0, 8, gram, 0)

    sib = (ga_at(zl, x, 1 - c), b)
    move = remote(part.at[:, pl.ds((1 - c) * 4, 4)], core_in, s_send.at[0], s_recv.at[0], sib)
    move.start()
    move.wait()
    mid[...] = part[:, pl.ds(c * 4, 4)] + core_in[...]

    moves = [
        remote(mid.at[:, (x + d) % 4], x_in.at[d - 1], s_send.at[d], s_recv.at[d], (ga_at(zl, (x + d) % 4, c), b))
        for d in range(1, 4)
    ]
    for move in moves:
        move.start()
    for move in moves:
        move.wait()
    low[...] = mid[:, x] + x_in[0] + x_in[1] + x_in[2]

    moves = [
        remote(
            low.at[:, pl.ds(((zl + d) % 4) * 16, 16)],
            z_in.at[d - 1],
            s_send.at[3 + d],
            s_recv.at[3 + d],
            (ga_at((zl + d) % 4, x, c), b),
        )
        for d in range(1, 4)
    ]
    for move in moves:
        move.start()
    for move in moves:
        move.wait()
    blk = c * 4 + x
    full[:, blk, b, zl] = low[:, pl.ds(zl * 16, 16)] + z_in[0] + z_in[1] + z_in[2]

    x_own()
    x_partner()

    def spread(view, base, devices):
        moves = [
            remote(view, view, s_send.at[base + n], s_recv.at[base + n], device) for n, device in enumerate(devices)
        ]
        for move in moves:
            move.start()
        for move in moves:
            move.wait()

    spread(full.at[:, blk, b, zl], 7, [(g, (b + d) % 8) for d in range(1, 8)])
    spread(full.at[:, blk, :, zl], 14, [(ga_at((zl + d) % 4, x, c), b) for d in range(1, 4)])
    spread(full.at[:, blk], 17, [(ga_at(zl, (x + d) % 4, c), b) for d in range(1, 4)])
    spread(full.at[:, pl.ds(c * 4, 4)], 20, [sib])

    out_t = pltpu.make_async_copy(gt, gt_ref, local_sem.at[0])
    out_f = pltpu.make_async_copy(full, full_ref, local_sem.at[1])
    out_t.start()
    out_f.start()
    x_far()
    x_finish()
    x_drain()
    out_t.wait()
    out_f.wait()


def exchange(trial, rest, scale):
    vmem = pl.BlockSpec(memory_space=pltpu.VMEM)
    anywhere = pl.BlockSpec(memory_space=pl.ANY)
    sem = pltpu.SemaphoreType.DMA
    return pl.pallas_call(
        functools.partial(exchange_kernel, scale),
        out_shape=(
            jax.ShapeDtypeStruct((8, 128, 1024), BF16),
            jax.ShapeDtypeStruct((8, 256, 1024), BF16),
            jax.ShapeDtypeStruct((2, 8, 8, 4, 16, 128), F32),
        ),
        in_specs=[vmem, vmem],
        out_specs=(anywhere, anywhere, anywhere),
        scratch_shapes=[
            pltpu.VMEM((8, 128, 1024), BF16),
            pltpu.VMEM((2, 8, 64, 128), F32),
            pltpu.VMEM((2, 4, 64, 128), F32),
            pltpu.VMEM((2, 4, 64, 128), F32),
            pltpu.VMEM((3, 2, 64, 128), F32),
            pltpu.VMEM((2, 64, 128), F32),
            pltpu.VMEM((3, 2, 16, 128), F32),
            pltpu.VMEM((2, 8, 8, 4, 16, 128), F32),
            sem((9,)),
            sem((9,)),
            sem((9,)),
            sem((9,)),
            sem((21,)),
            sem((21,)),
            sem((2,)),
        ],
        compiler_params=pltpu.CompilerParams(
            collective_id=0, has_side_effects=True, vmem_limit_bytes=48 * 2**20
        ),
    )(trial, rest)


def invert_pivot(block):
    lane, row = iota((64, 128), 1), iota((64, 128), 0)
    one = lane[:1]
    for k in range(0, 64, 2):
        m = k + 1
        c0r = jnp.broadcast_to(block[:, k : k + 1], (64, 128))
        c0i = jnp.broadcast_to(block[:, 64 + k : 65 + k], (64, 128))
        c1r = jnp.broadcast_to(block[:, m : m + 1], (64, 128))
        c1i = jnp.broadcast_to(block[:, 64 + m : 65 + m], (64, 128))
        r0, r1 = block[k : k + 1, :], block[m : m + 1, :]
        s0, s1 = pltpu.roll(r0, 64, 1), pltpu.roll(r1, 64, 1)
        s0, s1 = jnp.where(one < 64, -s0, s0), jnp.where(one < 64, -s1, s1)
        a, br, bi, c = c0r[k : k + 1], c1r[k : k + 1], c1i[k : k + 1], c1r[m : m + 1]
        e0, e0i, e1, e1i = one == k, one == 64 + k, one == m, one == 64 + m
        r0 = jnp.where(e0, 1.0, jnp.where(e0i | e1 | e1i, 0.0, r0))
        s0 = jnp.where(e0i, 1.0, jnp.where(e0 | e1 | e1i, 0.0, s0))
        r1 = jnp.where(e1, 1.0, jnp.where(e1i | e0 | e0i, 0.0, r1))
        s1 = jnp.where(e1i, 1.0, jnp.where(e1 | e0 | e0i, 0.0, s1))
        ra = 1.0 / a
        tr, ti = br * ra, bi * ra
        rs = 1.0 / (c - (br * br + bi * bi) * ra)
        i01r, i01i = -tr * rs, -ti * rs
        i00 = ra + (tr * tr + ti * ti) * rs
        q0 = i00 * r0 + i01r * r1 + i01i * s1
        q1 = i01r * r0 - i01i * s0 + rs * r1
        u0 = i00 * s0 + i01r * s1 - i01i * r1
        u1 = i01r * s0 + i01i * r0 + rs * s1
        isk, ism = row == k, row == m
        c0r = jnp.where(isk, -1.0, jnp.where(ism, 0.0, c0r))
        c1r = jnp.where(ism, -1.0, jnp.where(isk, 0.0, c1r))
        c0i, c1i = jnp.where(isk | ism, 0.0, c0i), jnp.where(isk | ism, 0.0, c1i)
        dead = isk | ism | (lane == k) | (lane == m) | (lane == 64 + k) | (lane == 64 + m)
        block = jnp.where(dead, 0.0, block) - c0r * q0 - c0i * u0 - c1r * q1 - c1i * u1
    return block


def halves(value):
    high = value.astype(BF16)
    return high, (value - high.astype(F32)).astype(BF16)


def dot(a, b):
    return jnp.dot(a, b, preferred_element_type=F32)


def dot_split(a, b):
    ah, al = halves(a)
    bh, bl = halves(b)
    return dot(ah, bh) + dot(al, bh) + dot(ah, bl)


def times_i(value):
    tiles = [pltpu.roll(value[:, n : n + 128], 64, 1) for n in range(0, value.shape[1], 128)]
    turned = jnp.concatenate(tiles, axis=1)
    return jnp.where(iota(value.shape, 1) % 128 < 64, -turned, turned)


def invert(work):
    def step(k, carry):
        rows, lanes = pl.ds(pl.multiple_of(k * 64, 64), 64), pl.ds(pl.multiple_of(k * 128, 128), 128)
        pivot = invert_pivot(work[rows, lanes])
        panel = work[rows, :]
        panel = dot_split(pivot, jnp.concatenate([panel, times_i(panel)], axis=0))
        panel = jnp.where(iota((64, 1024), 1) // 128 == k, jnp.concatenate([pivot] * 8, axis=1), panel)
        column = jnp.where(iota((512, 128), 0) // 64 == k, 0.0, work[:, lanes])
        work[:, lanes] = jnp.zeros((512, 128), F32)
        work[...] = work[...] - dot_split(column, jnp.concatenate([panel, times_i(panel)], axis=0))
        work[rows, :] = panel
        return carry

    lax.fori_loop(0, 8, step, 0)


def hermitian_part(full, m, out):
    lane = iota((64, 128), 1) < 64

    def row_block(k, carry):
        rows = pl.ds(pl.multiple_of(k * 64, 64), 64)
        for n in range(0, 8, 2):
            turned = full[m, k, pl.ds(64 * n, 128), :].T
            re, im = turned[0:64], -turned[64:128]
            left = jnp.where(lane, re, pltpu.roll(im, 64, 1))
            right = jnp.where(lane, pltpu.roll(re, 64, 1), im)
            out[rows, pl.ds(128 * n, 128)] = (full[m, n, rows, :] + left) * 0.5
            out[rows, pl.ds(128 * n + 128, 128)] = (full[m, n + 1, rows, :] + right) * 0.5
        return carry

    lax.fori_loop(0, 8, row_block, 0)


def expand(value_ref, high, low):
    def row_block(k, carry):
        rows = pl.ds(pl.multiple_of(k * 64, 64), 64)
        value = value_ref[rows, :]
        vh, vl = halves(value)
        th, tl = halves(times_i(value))
        top, bottom = pl.ds(pl.multiple_of(k * 128, 128), 64), pl.ds(pl.multiple_of(k * 128 + 64, 64), 64)
        high[top, :], high[bottom, :], low[top, :], low[bottom, :] = vh, th, vl, tl
        return carry

    lax.fori_loop(0, 8, row_block, 0)


def product(left_ref, rows, high, low, out):
    def column_block(n, carry):
        lanes = pl.ds(pl.multiple_of(n * 256, 256), 256)
        ah, al = halves(left_ref[rows, :])
        bh = high[:, lanes]
        out[:, lanes] = dot(ah, bh) + dot(al, bh) + dot(ah, low[:, lanes])
        return carry

    lax.fori_loop(0, 4, column_block, 0)


def fast_kernel(scale, t_ref, x_ref, gt_ref, gx_ref, z_ref, ok_ref, gt, part, core_in, mid, x_in, low, z_in, full,
                dcol, drow, e_left, right_a, right_b, one, two, three, four, t_send, t_recv, x_send, x_recv, s_send,
                s_recv, local_sem):
    g = lax.axis_index("ga")
    b = lax.axis_index("band")
    zl, x, c = g // 8, (g // 2) % 4, g % 2
    h, y = b // 4, b % 4
    partner = (1 - h) * 4 + y
    y_up, y_dn, y_far = (y + 1) % 4, (y + 3) % 4, (y + 2) % 4

    def band_at(hh, yy):
        return hh * 4 + yy

    def ga_at(zz, xx, cc):
        return zz * 8 + xx * 2 + cc

    bands = [(g, (b + d) % 8) for d in range(1, 8)]
    sib = (ga_at(zl, x, 1 - c), b)
    xs = [(ga_at(zl, (x + d) % 4, c), b) for d in range(1, 4)]
    zs = [(ga_at((zl + d) % 4, x, c), b) for d in range(1, 4)]
    barrier = pltpu.get_barrier_semaphore()
    greet = bands + [sib] + xs + zs
    for device in greet:
        pl.semaphore_signal(barrier, inc=1, device_id=device, device_id_type=MESH)
    pl.semaphore_wait(barrier, len(greet))

    up, dn, over = (g, band_at(h, y_up)), (g, band_at(h, y_dn)), (g, partner)
    b_dn, b_up, b_far = band_at(h, y_dn), band_at(h, y_up), band_at(h, y_far)
    p_dn, p_up, p_far = band_at(1 - h, y_dn), band_at(1 - h, y_up), band_at(1 - h, y_far)

    def gather(own, slots, size, send, recv):
        def move(n, src, block, rows, device):
            return remote(src, slots.at[block, rows], send.at[n], recv.at[n], device)

        def relay(n, block, rows, device):
            return move(n, slots.at[block, rows], block, rows, device)

        step = size // 4
        piece = [pl.ds(n * step, step) for n in range(4)]
        whole, lo, hi = pl.ds(0, size), pl.ds(0, size // 2), pl.ds(size // 2, size // 2)
        cross = [move(n, own.at[piece[n]], b, piece[n], over) for n in range(4)]
        near = [move(4, own, b, whole, up), move(5, own, b, whole, dn)]
        far = [relay(6, b_dn, lo, up), relay(7, b_up, hi, dn)]
        to_up = [relay(8 + n, partner, piece[n], up) for n in range(4)]
        to_dn = [relay(12 + n, partner, piece[n], dn) for n in range(4)]
        last = [relay(16, p_dn, piece[0], up), relay(17, p_dn, piece[1], up)]
        last += [relay(18, p_up, piece[2], dn), relay(19, p_up, piece[3], dn)]

        def start():
            cross[0].start()
            for copy in near + cross[1:]:
                copy.start()

        def pass_own():
            near[0].wait_recv()
            far[0].start()
            near[1].wait_recv()
            far[1].start()

        def pass_cross(n):
            cross[n].wait_recv()
            to_up[n].start()
            to_dn[n].start()

        def pass_last(n):
            (to_up if n < 2 else to_dn)[n].wait_recv()
            last[n].start()

        def finish():
            for copy in far + to_up[2:] + to_dn[:2] + last:
                copy.wait_recv()

        def drain():
            for copy in cross + near + far + to_up + to_dn + last:
                copy.wait_send()

        return start, pass_own, pass_cross, pass_last, finish, drain

    t_start, t_own, t_cross, t_last, t_finish, t_drain = gather(t_ref, gt, 128, t_send, t_recv)
    x_start, x_own, x_cross, x_last, x_finish, x_drain = gather(x_ref, gx_ref, 256, x_send, x_recv)

    sign = jnp.where(iota((64, 128), 1) < 64, scale, -scale).astype(F32)

    def gram(k, block):
        u = lax.dot_general(x_ref[...], block, (((1,), (1,)), ((), ())), preferred_element_type=F32)
        part[1, k] = u[0:64] * sign + pltpu.roll(u[64:128], 64, 1) * scale
        part[0, k] = u[128:192] * sign + pltpu.roll(u[192:256], 64, 1) * scale

    t_start()
    own_x = pltpu.make_async_copy(x_ref, gx_ref.at[b], local_sem.at[1])
    own_x.start()
    gt[b] = t_ref[...]
    gram(b, t_ref[...])
    t_cross(0)
    t_own()
    t_cross(1)
    t_last(0)
    t_cross(2)
    t_last(1)
    t_cross(3)
    gram(b_dn, gt[b_dn])
    gram(b_up, gt[b_up])
    gram(partner, gt[partner])
    t_last(2)
    t_last(3)
    t_finish()
    t_drain()
    x_start()
    for k in (b_far, p_dn, p_up, p_far):
        gram(k, gt[k])
    out_t = pltpu.make_async_copy(gt, gt_ref, local_sem.at[0])
    out_t.start()

    blk = c * 4 + x

    def core_moves(m):
        return [remote(part.at[m, pl.ds((1 - c) * 4, 4)], core_in.at[m], s_send.at[m, 0], s_recv.at[m, 0], sib)]

    def core_add(m):
        mid[m] = part[m, pl.ds(c * 4, 4)] + core_in[m]

    def x_moves(m):
        return [
            remote(mid.at[m, (x + d) % 4], x_in.at[m, d - 1], s_send.at[m, d], s_recv.at[m, d], xs[d - 1])
            for d in range(1, 4)
        ]

    def x_add(m):
        low[m] = mid[m, x] + x_in[m, 0] + x_in[m, 1] + x_in[m, 2]

    def z_moves(m):
        return [
            remote(
                low.at[m, pl.ds(((zl + d) % 4) * 16, 16)],
                z_in.at[m, d - 1],
                s_send.at[m, 3 + d],
                s_recv.at[m, 3 + d],
                zs[d - 1],
            )
            for d in range(1, 4)
        ]

    def z_add(m):
        piece = low[m, pl.ds(zl * 16, 16)] + z_in[m, 0] + z_in[m, 1] + z_in[m, 2]
        turned = pltpu.roll(piece, 64, 1)
        rest = turned - turned.astype(BF16).astype(F32)
        spot = (iota((16, 128), 1) == 64 + 16 * zl + iota((16, 128), 0)) & (blk == b)
        full[m, blk, b, zl] = jnp.where(spot, rest, piece).astype(BF16)

    def spread(m, view, base, devices):
        return [
            remote(view, view, s_send.at[m, base + n], s_recv.at[m, base + n], device)
            for n, device in enumerate(devices)
        ]

    stages = [
        (core_moves, core_add),
        (x_moves, x_add),
        (z_moves, z_add),
        (lambda m: spread(m, full.at[m, blk, b, zl], 7, bands), None),
        (lambda m: spread(m, full.at[m, blk, :, zl], 14, zs), None),
        (lambda m: spread(m, full.at[m, blk], 17, xs), None),
        (lambda m: spread(m, full.at[m, pl.ds(c * 4, 4)], 20, [sib]), None),
    ]
    flight = {}

    def launch(n, m):
        flight[n, m] = stages[n][0](m)
        for move in flight[n, m]:
            move.start()

    def land(n, m):
        for move in flight[n, m]:
            move.wait()
        if stages[n][1] is not None:
            stages[n][1](m)

    def turn(n):
        land(n, 0)
        launch(n + 1, 0)
        land(n, 1)
        launch(n + 1, 1)

    launch(0, 0)
    launch(0, 1)
    turn(0)
    turn(1)
    turn(2)
    x_own()
    x_cross(0)
    turn(3)
    x_cross(1)
    turn(4)
    x_cross(2)
    x_last(0)
    turn(5)
    x_cross(3)
    x_last(1)
    land(6, 0)

    lane64 = iota((64, 128), 1) < 64
    eye = iota((64, 128), 0) == iota((64, 128), 1)

    def tile(m, n, k, count):
        return full[m, n, pl.ds(k, count)].astype(F32).reshape(64 * count, 128)

    def scales(k, carry):
        rows = pl.ds(pl.multiple_of(k * 64, 64), 64)
        block = tile(0, k, k, 1)
        diagonal = jnp.where(eye, block + pltpu.roll(block, 64, 1), 0.0)
        dcol[rows, :] = jnp.broadcast_to(lax.rsqrt(jnp.sum(diagonal, axis=1, keepdims=True)), (64, 128))
        across = jnp.sum(diagonal, axis=0, keepdims=True)
        across = lax.rsqrt(across + pltpu.roll(across, 64, 1))
        drow[:, pl.ds(pl.multiple_of(k * 128, 128), 128)] = jnp.broadcast_to(across, (8, 128))
        return carry

    lax.fori_loop(0, 8, scales, 0)

    def scaled_part(m, out, factor, diagonal):
        def row_block(k, carry):
            rows = pl.ds(pl.multiple_of(k * 64, 64), 64)
            left = dcol[rows, :] * (0.5 * factor)
            for n in range(0, 8, 2):
                turned = tile(m, k, n, 2).T
                re, im = turned[0:64], -turned[64:128]
                back = (
                    jnp.where(lane64, re, pltpu.roll(im, 64, 1)),
                    jnp.where(lane64, pltpu.roll(re, 64, 1), im),
                )
                for i in range(2):
                    lanes = pl.ds(128 * (n + i), 128)
                    block = tile(m, n + i, k, 1)
                    value = (block + back[i]) * left * drow[0:1, lanes]
                    out[rows, lanes] = diagonal(value, k, n + i, left, drow[0:1, lanes], block)
            return carry

        lax.fori_loop(0, 8, row_block, 0)

    spot_im = iota((64, 128), 0) + 64 == iota((64, 128), 1)

    def no_diagonal(value, k, n, left, right, block):
        return jnp.where((eye | spot_im) & (k == n), 0.0, value)

    def full_diagonal(value, k, n, left, right, block):
        exact = (block + pltpu.roll(block, 64, 1)) * 2.0 * left * right
        value = jnp.where(eye & (k == n), exact, value)
        return jnp.where(spot_im & (k == n), 0.0, value)

    def put_right(right, lanes, value):
        turned = times_i(value)
        for k in range(8):
            rows = slice(64 * k, 64 * k + 64)
            right[pl.ds(128 * k, 64), lanes] = value[rows].astype(BF16)
            right[pl.ds(128 * k + 64, 64), lanes] = turned[rows].astype(BF16)

    def by_columns(body, init=0):
        def column_block(n, carry):
            return body(pl.ds(pl.multiple_of(n * 256, 256), 256), carry)

        return lax.fori_loop(0, 4, column_block, init)

    def square_sum(value):
        return jnp.sum(value, axis=0, keepdims=True)

    zero_row = jnp.zeros((1, 256), F32)
    scaled_part(0, one, -1.0, no_diagonal)

    def prepare(lanes, carry):
        value = one[:, lanes]
        e_left[:, lanes] = value.astype(BF16)
        put_right(right_a, lanes, value)
        return carry

    by_columns(prepare)

    def second_power(lanes, carry):
        value = dot(e_left[...], right_a[:, lanes])
        two[:, lanes] = value
        put_right(right_b, lanes, value + one[:, lanes])
        return carry

    by_columns(second_power)

    def third_power(lanes, carry):
        value = dot(e_left[...], right_b[:, lanes])
        cube = value - two[:, lanes]
        three[:, lanes] = cube
        one[:, lanes] = one[:, lanes] + value
        return carry + square_sum(cube * cube)

    cube_norm = by_columns(third_power, zero_row)
    land(6, 1)
    x_last(2)
    x_last(3)
    scaled_part(1, four, 1.0, full_diagonal)
    e_left[...] = three[...].astype(BF16)

    def series(lanes, carry):
        value = one[:, lanes] + dot(e_left[...], right_b[:, lanes])
        two[:, lanes] = value
        put_right(right_a, lanes, value)
        return carry

    by_columns(series)

    def ham_right(lanes, carry):
        e_left[:, lanes] = two[:, lanes].astype(BF16)
        put_right(right_b, lanes, four[:, lanes])
        return carry

    by_columns(ham_right)

    def first_product(lanes, carry):
        one[:, lanes] = four[:, lanes] + dot(e_left[...], right_b[:, lanes])
        return carry

    by_columns(first_product)
    e_left[...] = one[...].astype(BF16)

    def second_product(lanes, carry):
        value = one[:, lanes] + dot(e_left[...], right_a[:, lanes])
        three[:, lanes] = value
        put_right(right_b, lanes, value)
        return (carry[0] + square_sum(value * four[:, lanes]), carry[1] + square_sum(value * one[:, lanes]))

    sums = by_columns(second_product, (zero_row, zero_row))
    trace_qh = jnp.sum(sums[0], keepdims=True)
    trace_pq = jnp.sum(sums[1], keepdims=True)
    rs = lax.rsqrt(jnp.maximum(trace_qh, 0.0) * (1.0 / 512) + 1e-6)
    own = pl.ds(pl.multiple_of(b * 64, 64), 64)
    own_lanes = pl.ds(pl.multiple_of(b * 128, 128), 128)
    product = dot(e_left[own, :], right_b[...])
    z = two[own, :] - three[own, :] * rs + product * (0.25 * rs * rs)
    four[own, :] = z
    four[own, own_lanes] = four[own, own_lanes] + jnp.where(eye, 1.0, 0.0)
    left = jnp.concatenate([dcol[own, :]] * 8, axis=1)
    z_ref[...] = (four[own, :] * left * drow[0:1, :]).astype(BF16)

    def trace_of(ref):
        def row_block(k, carry):
            block = ref[pl.ds(pl.multiple_of(k * 64, 64), 64), pl.ds(pl.multiple_of(k * 128, 128), 128)]
            return carry + jnp.where(eye, block, 0.0)

        return jnp.sum(lax.fori_loop(0, 8, row_block, jnp.zeros((64, 128), F32)), keepdims=True)

    trace_w = 512.0 + trace_of(two)
    trace_z = trace_w - trace_of(three) * rs + trace_pq * (0.25 * rs * rs)
    small = jnp.sum(cube_norm, keepdims=True) < 0.0225
    ok = small & (trace_z > 0.6 * trace_w)
    ok_ref[...] = jnp.broadcast_to(jnp.where(ok, 1, 0).astype(jnp.int32), (8, 128))

    x_finish()
    x_drain()
    own_x.wait()
    out_t.wait()


def fast_filter(trial, rest, scale):
    vmem = pl.BlockSpec(memory_space=pltpu.VMEM)
    anywhere = pl.BlockSpec(memory_space=pl.ANY)
    sem = pltpu.SemaphoreType.DMA
    square = pltpu.VMEM((512, 1024), F32)
    return pl.pallas_call(
        functools.partial(fast_kernel, scale),
        out_shape=(
            jax.ShapeDtypeStruct((8, 128, 1024), BF16),
            jax.ShapeDtypeStruct((8, 256, 1024), BF16),
            jax.ShapeDtypeStruct((64, 1024), BF16),
            jax.ShapeDtypeStruct((8, 128), jnp.int32),
        ),
        in_specs=[vmem, vmem],
        out_specs=(anywhere, anywhere, vmem, vmem),
        scratch_shapes=[
            pltpu.VMEM((8, 128, 1024), BF16),
            pltpu.VMEM((2, 8, 64, 128), F32),
            pltpu.VMEM((2, 4, 64, 128), F32),
            pltpu.VMEM((2, 4, 64, 128), F32),
            pltpu.VMEM((2, 3, 64, 128), F32),
            pltpu.VMEM((2, 64, 128), F32),
            pltpu.VMEM((2, 3, 16, 128), F32),
            pltpu.VMEM((2, 8, 8, 4, 16, 128), BF16),
            pltpu.VMEM((512, 128), F32),
            pltpu.VMEM((8, 1024), F32),
            pltpu.VMEM((512, 1024), BF16),
            pltpu.VMEM((1024, 1024), BF16),
            pltpu.VMEM((1024, 1024), BF16),
            square,
            square,
            square,
            square,
            sem((20,)),
            sem((20,)),
            sem((20,)),
            sem((20,)),
            sem((2, 21)),
            sem((2, 21)),
            sem((2,)),
        ],
        compiler_params=pltpu.CompilerParams(
            collective_id=1, has_side_effects=True, vmem_limit_bytes=48 * 2**20
        ),
    )(trial, rest)


def turn_blocks(z, gt, gx, o_ref):
    turned = times_i(z)
    re_part = jnp.where(iota((64, 1024), 1) % 128 < 64, z, -z)
    im_part = jnp.where(iota((64, 1024), 1) % 128 < 64, -turned, turned)
    weights = jnp.concatenate([re_part, im_part], axis=0).astype(BF16)
    o_ref[0] = dot(weights, gt[...].reshape(1024, 1024)).astype(BF16)
    o_ref[1] = dot(weights, gx[:, 0:128, :].reshape(1024, 1024)).astype(BF16)
    o_ref[2] = dot(weights, gx[:, 128:256, :].reshape(1024, 1024)).astype(BF16)


def fast_rotate_kernel(z_ref, gt, gx, o_ref):
    turn_blocks(z_ref[...].astype(F32), gt, gx, o_ref)


def fast_rotate(z, gt, gx):
    vmem = pl.BlockSpec(memory_space=pltpu.VMEM)
    return pl.pallas_call(
        fast_rotate_kernel,
        out_shape=jax.ShapeDtypeStruct((3, 128, 1024), BF16),
        in_specs=[vmem] * 3,
        out_specs=vmem,
        compiler_params=pltpu.CompilerParams(vmem_limit_bytes=48 * 2**20),
    )(z, gt, gx)


def rotate_kernel(full, gt, gx, o_ref, w, ham, p, q, pq, high, low):
    b = lax.axis_index("band")
    own = pl.ds(pl.multiple_of(b * 64, 64), 64)
    hermitian_part(full, 0, w)
    hermitian_part(full, 1, ham)
    invert(w)
    expand(ham, high, low)
    product(w, pl.ds(0, 512), high, low, p)
    expand(w, high, low)
    product(p, pl.ds(0, 512), high, low, q)
    total = jnp.sum(q[...] * ham[...], keepdims=True)
    rs = lax.rsqrt(jnp.maximum(total, 0.0) * (1.0 / 512) + 1e-6)
    expand(q, high, low)
    product(p, own, high, low, pq)
    z = w[own, :] - q[own, :] * rs + pq[...] * (0.25 * rs * rs)
    turn_blocks(z.astype(BF16).astype(F32), gt, gx, o_ref)


def rotate(full, gt, gx):
    vmem = pl.BlockSpec(memory_space=pltpu.VMEM)
    return pl.pallas_call(
        rotate_kernel,
        out_shape=jax.ShapeDtypeStruct((3, 128, 1024), BF16),
        in_specs=[vmem] * 3,
        out_specs=vmem,
        scratch_shapes=[
            pltpu.VMEM((512, 1024), F32),
            pltpu.VMEM((512, 1024), F32),
            pltpu.VMEM((512, 1024), F32),
            pltpu.VMEM((512, 1024), F32),
            pltpu.VMEM((64, 1024), F32),
            pltpu.VMEM((1024, 1024), BF16),
            pltpu.VMEM((1024, 1024), BF16),
        ],
        compiler_params=pltpu.CompilerParams(vmem_limit_bytes=48 * 2**20),
    )(full, gt, gx)


def local(trial, applied, extra):
    margin = (trial.astype(F32) + extra.astype(F32)).astype(BF16)
    rows, _, length = trial.shape

    def planes(block):
        return jnp.swapaxes(block, 0, 1).reshape(2 * rows, length)

    rest = jnp.concatenate([planes(applied), planes(margin)], axis=0)
    scale = 1.0 / (length * lax.axis_size("ga"))
    own = planes(trial)
    gt, gx, z, ok = fast_filter(own, rest, scale)

    def direct():
        blocks, others, full = exchange(own, rest, scale)
        return rotate(full.reshape(2, 8, 512, 128), blocks, others)

    out = lax.cond(ok[0, 0] > 0, lambda: fast_rotate(z, gt, gx), direct)
    out = out.reshape(3, 2, rows, length)
    return tuple(jnp.swapaxes(out[n], 0, 1) for n in range(3))


def solution(mesh):
    spec = P("band", None, "ga")
    return jax.shard_map(local, mesh=mesh, in_specs=(spec,) * 3, out_specs=(spec,) * 3, check_vma=False)
```

```python
import functools

import jax
import jax.numpy as jnp
from jax import lax
from jax.experimental import pallas as pl
from jax.experimental.pallas import tpu as pltpu
from jax.sharding import PartitionSpec as P

MESH = pl.DeviceIdType.MESH
F32 = jnp.float32
BF16 = jnp.bfloat16


def iota(shape, dim):
    return lax.broadcasted_iota(jnp.int32, shape, dim)


def remote(src, dst, send_sem, recv_sem, device):
    return pltpu.make_async_remote_copy(
        src_ref=src,
        dst_ref=dst,
        send_sem=send_sem,
        recv_sem=recv_sem,
        device_id=device,
        device_id_type=MESH,
    )


def exchange_kernel(scale, t_ref, x_ref, gt_ref, gx_ref, full_ref, gt, part, core_in, mid, x_in, low, z_in, full,
                    t_send, t_recv, x_send, x_recv, s_send, s_recv, local_sem):
    g = lax.axis_index("ga")
    b = lax.axis_index("band")
    zl, x, c = g // 8, (g // 2) % 4, g % 2
    h, y = b // 4, b % 4
    partner = (1 - h) * 4 + y
    y_up, y_dn, y_far = (y + 1) % 4, (y + 3) % 4, (y + 2) % 4

    def band_at(hh, yy):
        return hh * 4 + yy

    def ga_at(zz, xx, cc):
        return zz * 8 + xx * 2 + cc

    barrier = pltpu.get_barrier_semaphore()
    greet = [(g, (b + d) % 8) for d in range(1, 8)]
    greet += [(ga_at(zl, x, 1 - c), b)]
    greet += [(ga_at(zl, (x + d) % 4, c), b) for d in range(1, 4)]
    greet += [(ga_at((zl + d) % 4, x, c), b) for d in range(1, 4)]
    for device in greet:
        pl.semaphore_signal(barrier, inc=1, device_id=device, device_id_type=MESH)
    pl.semaphore_wait(barrier, len(greet))

    up, dn, over = (g, band_at(h, y_up)), (g, band_at(h, y_dn)), (g, partner)

    def gather(own, slots, half, send, recv):
        def move(n, src, block, rows, device):
            return remote(src, slots.at[block, rows], send.at[n], recv.at[n], device)

        whole = pl.ds(0, 2 * half)
        lo, hi = pl.ds(0, half), pl.ds(half, half)
        b_dn, b_up = band_at(h, y_dn), band_at(h, y_up)
        p_dn, p_up = band_at(1 - h, y_dn), band_at(1 - h, y_up)
        first = [move(0, own, b, whole, over), move(1, own, b, whole, up), move(2, own, b, whole, dn)]
        second = [
            move(3, slots.at[partner], partner, whole, up),
            move(4, slots.at[partner], partner, whole, dn),
            move(5, slots.at[b_dn, lo], b_dn, lo, up),
            move(6, slots.at[b_up, hi], b_up, hi, dn),
            move(7, slots.at[p_dn, lo], p_dn, lo, up),
            move(8, slots.at[p_up, hi], p_up, hi, dn),
        ]

        def start():
            for copy in first:
                copy.start()

        def forward_own():
            first[1].wait_recv()
            second[2].start()
            first[2].wait_recv()
            second[3].start()

        def forward_partner():
            first[0].wait_recv()
            second[0].start()
            second[1].start()

        def forward_far():
            second[0].wait_recv()
            second[4].start()
            second[1].wait_recv()
            second[5].start()

        def finish():
            for copy in second[2:]:
                copy.wait_recv()

        def drain():
            for copy in first + second:
                copy.wait_send()

        return start, forward_own, forward_partner, forward_far, finish, drain

    t_start, t_own, t_partner, t_far, t_finish, t_drain = gather(t_ref, gt, 64, t_send, t_recv)
    x_start, x_own, x_partner, x_far, x_finish, x_drain = gather(x_ref, gx_ref, 128, x_send, x_recv)
    t_start()
    own_t = pltpu.make_async_copy(t_ref, gt.at[b], local_sem.at[0])
    own_t.start()
    own_x = pltpu.make_async_copy(x_ref, gx_ref.at[b], local_sem.at[1])
    own_x.start()
    own_t.wait()
    own_x.wait()
    t_own()
    t_partner()
    t_far()
    t_finish()
    t_drain()
    x_start()

    sign = jnp.where(iota((64, 128), 1) < 64, scale, -scale).astype(F32)

    def gram(k, carry):
        u = lax.dot_general(
            x_ref[...], gt[k], (((1,), (1,)), ((), ())), preferred_element_type=F32
        )
        part[1, k] = u[0:64] * sign + pltpu.roll(u[64:128], 64, 1) * scale
        part[0, k] = u[128:192] * sign + pltpu.roll(u[192:256], 64, 1) * scale
        return carry

    lax.fori_loop(0, 8, gram, 0)

    sib = (ga_at(zl, x, 1 - c), b)
    move = remote(part.at[:, pl.ds((1 - c) * 4, 4)], core_in, s_send.at[0], s_recv.at[0], sib)
    move.start()
    move.wait()
    mid[...] = part[:, pl.ds(c * 4, 4)] + core_in[...]

    moves = [
        remote(mid.at[:, (x + d) % 4], x_in.at[d - 1], s_send.at[d], s_recv.at[d], (ga_at(zl, (x + d) % 4, c), b))
        for d in range(1, 4)
    ]
    for move in moves:
        move.start()
    for move in moves:
        move.wait()
    low[...] = mid[:, x] + x_in[0] + x_in[1] + x_in[2]

    moves = [
        remote(
            low.at[:, pl.ds(((zl + d) % 4) * 16, 16)],
            z_in.at[d - 1],
            s_send.at[3 + d],
            s_recv.at[3 + d],
            (ga_at((zl + d) % 4, x, c), b),
        )
        for d in range(1, 4)
    ]
    for move in moves:
        move.start()
    for move in moves:
        move.wait()
    blk = c * 4 + x
    full[:, blk, b, zl] = low[:, pl.ds(zl * 16, 16)] + z_in[0] + z_in[1] + z_in[2]

    x_own()
    x_partner()

    def spread(view, base, devices):
        moves = [
            remote(view, view, s_send.at[base + n], s_recv.at[base + n], device) for n, device in enumerate(devices)
        ]
        for move in moves:
            move.start()
        for move in moves:
            move.wait()

    spread(full.at[:, blk, b, zl], 7, [(g, (b + d) % 8) for d in range(1, 8)])
    spread(full.at[:, blk, :, zl], 14, [(ga_at((zl + d) % 4, x, c), b) for d in range(1, 4)])
    spread(full.at[:, blk], 17, [(ga_at(zl, (x + d) % 4, c), b) for d in range(1, 4)])
    spread(full.at[:, pl.ds(c * 4, 4)], 20, [sib])

    out_t = pltpu.make_async_copy(gt, gt_ref, local_sem.at[0])
    out_f = pltpu.make_async_copy(full, full_ref, local_sem.at[1])
    out_t.start()
    out_f.start()
    x_far()
    x_finish()
    x_drain()
    out_t.wait()
    out_f.wait()


def exchange(trial, rest, scale):
    vmem = pl.BlockSpec(memory_space=pltpu.VMEM)
    anywhere = pl.BlockSpec(memory_space=pl.ANY)
    sem = pltpu.SemaphoreType.DMA
    return pl.pallas_call(
        functools.partial(exchange_kernel, scale),
        out_shape=(
            jax.ShapeDtypeStruct((8, 128, 1024), BF16),
            jax.ShapeDtypeStruct((8, 256, 1024), BF16),
            jax.ShapeDtypeStruct((2, 8, 8, 4, 16, 128), F32),
        ),
        in_specs=[vmem, vmem],
        out_specs=(anywhere, anywhere, anywhere),
        scratch_shapes=[
            pltpu.VMEM((8, 128, 1024), BF16),
            pltpu.VMEM((2, 8, 64, 128), F32),
            pltpu.VMEM((2, 4, 64, 128), F32),
            pltpu.VMEM((2, 4, 64, 128), F32),
            pltpu.VMEM((3, 2, 64, 128), F32),
            pltpu.VMEM((2, 64, 128), F32),
            pltpu.VMEM((3, 2, 16, 128), F32),
            pltpu.VMEM((2, 8, 8, 4, 16, 128), F32),
            sem((9,)),
            sem((9,)),
            sem((9,)),
            sem((9,)),
            sem((21,)),
            sem((21,)),
            sem((2,)),
        ],
        compiler_params=pltpu.CompilerParams(
            collective_id=0, has_side_effects=True, vmem_limit_bytes=48 * 2**20
        ),
    )(trial, rest)


def invert_pivot(block):
    lane, row = iota((64, 128), 1), iota((64, 128), 0)
    one = lane[:1]
    for k in range(0, 64, 2):
        m = k + 1
        c0r = jnp.broadcast_to(block[:, k : k + 1], (64, 128))
        c0i = jnp.broadcast_to(block[:, 64 + k : 65 + k], (64, 128))
        c1r = jnp.broadcast_to(block[:, m : m + 1], (64, 128))
        c1i = jnp.broadcast_to(block[:, 64 + m : 65 + m], (64, 128))
        r0, r1 = block[k : k + 1, :], block[m : m + 1, :]
        s0, s1 = pltpu.roll(r0, 64, 1), pltpu.roll(r1, 64, 1)
        s0, s1 = jnp.where(one < 64, -s0, s0), jnp.where(one < 64, -s1, s1)
        a, br, bi, c = c0r[k : k + 1], c1r[k : k + 1], c1i[k : k + 1], c1r[m : m + 1]
        e0, e0i, e1, e1i = one == k, one == 64 + k, one == m, one == 64 + m
        r0 = jnp.where(e0, 1.0, jnp.where(e0i | e1 | e1i, 0.0, r0))
        s0 = jnp.where(e0i, 1.0, jnp.where(e0 | e1 | e1i, 0.0, s0))
        r1 = jnp.where(e1, 1.0, jnp.where(e1i | e0 | e0i, 0.0, r1))
        s1 = jnp.where(e1i, 1.0, jnp.where(e1 | e0 | e0i, 0.0, s1))
        ra = 1.0 / a
        tr, ti = br * ra, bi * ra
        rs = 1.0 / (c - (br * br + bi * bi) * ra)
        i01r, i01i = -tr * rs, -ti * rs
        i00 = ra + (tr * tr + ti * ti) * rs
        q0 = i00 * r0 + i01r * r1 + i01i * s1
        q1 = i01r * r0 - i01i * s0 + rs * r1
        u0 = i00 * s0 + i01r * s1 - i01i * r1
        u1 = i01r * s0 + i01i * r0 + rs * s1
        isk, ism = row == k, row == m
        c0r = jnp.where(isk, -1.0, jnp.where(ism, 0.0, c0r))
        c1r = jnp.where(ism, -1.0, jnp.where(isk, 0.0, c1r))
        c0i, c1i = jnp.where(isk | ism, 0.0, c0i), jnp.where(isk | ism, 0.0, c1i)
        dead = isk | ism | (lane == k) | (lane == m) | (lane == 64 + k) | (lane == 64 + m)
        block = jnp.where(dead, 0.0, block) - c0r * q0 - c0i * u0 - c1r * q1 - c1i * u1
    return block


def halves(value):
    high = value.astype(BF16)
    return high, (value - high.astype(F32)).astype(BF16)


def dot(a, b):
    return jnp.dot(a, b, preferred_element_type=F32)


def dot_split(a, b):
    ah, al = halves(a)
    bh, bl = halves(b)
    return dot(ah, bh) + dot(al, bh) + dot(ah, bl)


def times_i(value):
    tiles = [pltpu.roll(value[:, n : n + 128], 64, 1) for n in range(0, value.shape[1], 128)]
    turned = jnp.concatenate(tiles, axis=1)
    return jnp.where(iota(value.shape, 1) % 128 < 64, -turned, turned)


def invert(work):
    def step(k, carry):
        rows, lanes = pl.ds(pl.multiple_of(k * 64, 64), 64), pl.ds(pl.multiple_of(k * 128, 128), 128)
        pivot = invert_pivot(work[rows, lanes])
        panel = work[rows, :]
        panel = dot_split(pivot, jnp.concatenate([panel, times_i(panel)], axis=0))
        panel = jnp.where(iota((64, 1024), 1) // 128 == k, jnp.concatenate([pivot] * 8, axis=1), panel)
        column = jnp.where(iota((512, 128), 0) // 64 == k, 0.0, work[:, lanes])
        work[:, lanes] = jnp.zeros((512, 128), F32)
        work[...] = work[...] - dot_split(column, jnp.concatenate([panel, times_i(panel)], axis=0))
        work[rows, :] = panel
        return carry

    lax.fori_loop(0, 8, step, 0)


def hermitian_part(full, m, out):
    lane = iota((64, 128), 1) < 64

    def row_block(k, carry):
        rows = pl.ds(pl.multiple_of(k * 64, 64), 64)
        for n in range(0, 8, 2):
            turned = full[m, k, pl.ds(64 * n, 128), :].T
            re, im = turned[0:64], -turned[64:128]
            left = jnp.where(lane, re, pltpu.roll(im, 64, 1))
            right = jnp.where(lane, pltpu.roll(re, 64, 1), im)
            out[rows, pl.ds(128 * n, 128)] = (full[m, n, rows, :] + left) * 0.5
            out[rows, pl.ds(128 * n + 128, 128)] = (full[m, n + 1, rows, :] + right) * 0.5
        return carry

    lax.fori_loop(0, 8, row_block, 0)


def expand(value_ref, high, low):
    def row_block(k, carry):
        rows = pl.ds(pl.multiple_of(k * 64, 64), 64)
        value = value_ref[rows, :]
        vh, vl = halves(value)
        th, tl = halves(times_i(value))
        top, bottom = pl.ds(pl.multiple_of(k * 128, 128), 64), pl.ds(pl.multiple_of(k * 128 + 64, 64), 64)
        high[top, :], high[bottom, :], low[top, :], low[bottom, :] = vh, th, vl, tl
        return carry

    lax.fori_loop(0, 8, row_block, 0)


def product(left_ref, rows, high, low, out):
    def column_block(n, carry):
        lanes = pl.ds(pl.multiple_of(n * 256, 256), 256)
        ah, al = halves(left_ref[rows, :])
        bh = high[:, lanes]
        out[:, lanes] = dot(ah, bh) + dot(al, bh) + dot(ah, low[:, lanes])
        return carry

    lax.fori_loop(0, 4, column_block, 0)


def unweave(to_planes):
    row, col = iota((128, 128), 0), iota((128, 128), 1)
    if not to_planes:
        row, col = col, row
    source = jnp.where(row < 64, 2 * row, 2 * row - 127)
    return jnp.where(col == source, 1.0, 0.0).astype(BF16)


def fast_kernel(scale, trial, applied, extra, gt_ref, gx_ref, z_ref, ok_ref, t_ref, x_ref, gt, part, core_in, mid, x_in,
                ring, full, dcol, drow, left_a, left_b, right_a, right_b, right_c, one, two, three, four, t_send,
                t_recv, x_send, x_recv, s_send, s_recv, local_sem):
    g = lax.axis_index("ga")
    b = lax.axis_index("band")
    zl, x, c = g // 8, (g // 2) % 4, g % 2
    h, y = b // 4, b % 4
    partner = (1 - h) * 4 + y
    y_up, y_dn, y_far = (y + 1) % 4, (y + 3) % 4, (y + 2) % 4

    def band_at(hh, yy):
        return hh * 4 + yy

    def ga_at(zz, xx, cc):
        return zz * 8 + xx * 2 + cc

    def ring_at(d):
        z = (h * 4 + zl + d) % 8
        return (ga_at(z % 4, x, c), band_at(z // 4, y))

    sib = (ga_at(zl, x, 1 - c), b)
    xs = [(ga_at(zl, (x + d) % 4, c), b) for d in range(1, 4)]
    ys = [(g, band_at(h, (y + d) % 4)) for d in range(1, 4)]
    rings = [ring_at(d) for d in range(1, 8)]
    barrier = pltpu.get_barrier_semaphore()
    greet = [sib] + xs + ys + rings
    for device in greet:
        pl.semaphore_signal(barrier, inc=1, device_id=device, device_id_type=MESH)
    planes = unweave(True)
    t_ref[...] = dot(planes, trial[...].reshape(128, 1024)).astype(BF16)
    pl.semaphore_wait(barrier, len(greet))

    up, dn, over = (g, band_at(h, y_up)), (g, band_at(h, y_dn)), (g, partner)
    b_dn, b_up, b_far = band_at(h, y_dn), band_at(h, y_up), band_at(h, y_far)
    p_dn, p_up, p_far = band_at(1 - h, y_dn), band_at(1 - h, y_up), band_at(1 - h, y_far)

    class Gather:
        def __init__(self, own, slots, size, send, recv):
            def move(n, src, block, rows, device):
                return remote(src, slots.at[block, rows], send.at[n], recv.at[n], device)

            def relay(n, block, rows, device):
                return move(n, slots.at[block, rows], block, rows, device)

            step = size // 4
            piece = [pl.ds(n * step, step) for n in range(4)]
            whole, lo, hi = pl.ds(0, size), pl.ds(0, size // 2), pl.ds(size // 2, size // 2)
            self.cross = [move(n, own.at[piece[n]], b, piece[n], over) for n in range(4)]
            self.near = [move(4, own, b, whole, up), move(5, own, b, whole, dn)]
            self.far = [relay(6, b_dn, lo, up), relay(7, b_up, hi, dn)]
            self.to_up = [relay(8 + n, partner, piece[n], up) for n in range(4)]
            self.to_dn = [relay(12 + n, partner, piece[n], dn) for n in range(4)]
            self.last = [relay(16, p_dn, piece[0], up), relay(17, p_dn, piece[1], up)]
            self.last += [relay(18, p_up, piece[2], dn), relay(19, p_up, piece[3], dn)]

        def start_near(self):
            for copy in self.near:
                copy.start()

        def start_cross(self, first, count):
            for copy in self.cross[first : first + count]:
                copy.start()

        def pass_own(self):
            for n in range(2):
                self.near[n].wait_recv()
                self.far[n].start()

        def pass_cross(self, n):
            self.cross[n].wait_recv()
            self.to_up[n].start()
            self.to_dn[n].start()

        def pass_last(self, n):
            (self.to_up if n < 2 else self.to_dn)[n].wait_recv()
            self.last[n].start()

        def finish(self):
            for copy in self.far + self.to_up[2:] + self.to_dn[:2] + self.last:
                copy.wait_recv()

        def drain(self):
            for copy in self.cross + self.near + self.far + self.to_up + self.to_dn + self.last:
                copy.wait_send()

    tg = Gather(t_ref, gt, 128, t_send, t_recv)
    xg = Gather(x_ref, gx_ref, 256, x_send, x_recv)

    sign = jnp.where(iota((64, 128), 1) < 64, scale, -scale).astype(F32)

    def gram(k, block):
        u = lax.dot_general(x_ref[...], block, (((1,), (1,)), ((), ())), preferred_element_type=F32)
        part[1, k] = u[0:64] * sign + pltpu.roll(u[64:128], 64, 1) * scale
        part[0, k] = u[128:192] * sign + pltpu.roll(u[192:256], 64, 1) * scale

    tg.start_cross(0, 1)
    tg.start_near()
    tg.start_cross(1, 3)
    x_ref[0:128] = dot(planes, applied[...].reshape(128, 1024)).astype(BF16)
    margin = (trial[...].astype(F32) + extra[...].astype(F32)).astype(BF16)
    x_ref[128:256] = dot(planes, margin.reshape(128, 1024)).astype(BF16)
    own_x = pltpu.make_async_copy(x_ref, gx_ref.at[b], local_sem.at[1])
    own_x.start()
    gt[b] = t_ref[...]
    gram(b, t_ref[...])
    tg.pass_cross(0)
    tg.pass_own()
    tg.pass_cross(1)
    tg.pass_last(0)
    tg.pass_cross(2)
    tg.pass_last(1)
    tg.pass_cross(3)
    xg.start_cross(0, 2)
    gram(b_dn, gt[b_dn])
    gram(b_up, gt[b_up])
    gram(partner, gt[partner])
    tg.pass_last(2)
    tg.pass_last(3)
    tg.finish()
    xg.start_near()
    for k in (b_far, p_dn, p_up, p_far):
        gram(k, gt[k])

    blk = c * 4 + x
    lane64 = iota((64, 128), 1) < 64
    eye = iota((64, 128), 0) == iota((64, 128), 1)
    eye_im = iota((64, 128), 0) + 64 == iota((64, 128), 1)

    def rounded(value):
        return value.astype(BF16).astype(F32)

    def core_moves(m):
        return [remote(part.at[m, pl.ds((1 - c) * 4, 4)], core_in.at[m], s_send.at[m, 0], s_recv.at[m, 0], sib)]

    def core_add(m):
        mid[m] = part[m, pl.ds(c * 4, 4)] + core_in[m]

    def x_moves(m):
        return [
            remote(mid.at[m, (x + d) % 4], x_in.at[m, d - 1], s_send.at[m, d], s_recv.at[m, d], xs[d - 1])
            for d in range(1, 4)
        ]

    def x_add(m):
        value = mid[m, x] + x_in[m, 0] + x_in[m, 1] + x_in[m, 2]
        turned = pltpu.roll(value, 64, 1)
        ring[m, h, zl] = jnp.where(eye_im & (blk == b), turned - rounded(turned), value).astype(BF16)

    def spread(m, view, base, devices):
        return [
            remote(view, view, s_send.at[m, base + n], s_recv.at[m, base + n], device)
            for n, device in enumerate(devices)
        ]

    def ring_add(m):
        for hh in range(2):
            value = ring[m, hh, 0].astype(F32)
            for n in range(1, 4):
                value = value + ring[m, hh, n].astype(F32)
            exact = value + pltpu.roll(value, 64, 1)
            mine = blk == hh * 4 + y
            value = jnp.where(eye & mine, exact, jnp.where(eye_im & mine, exact - rounded(exact), value))
            full[m, blk, hh, y] = value.astype(BF16)

    stages = [
        (core_moves, core_add),
        (x_moves, x_add),
        (lambda m: spread(m, ring.at[m, h, zl], 4, rings), ring_add),
        (lambda m: spread(m, full.at[m, blk, :, y], 11, ys), None),
        (lambda m: spread(m, full.at[m, blk], 14, xs), None),
        (lambda m: spread(m, full.at[m, pl.ds(c * 4, 4)], 17, [sib]), None),
    ]
    flight = {}

    def launch(n, m):
        flight[n, m] = stages[n][0](m)
        for move in flight[n, m]:
            move.start()

    def land(n, m):
        for move in flight[n, m]:
            move.wait()
        if stages[n][1] is not None:
            stages[n][1](m)

    def turn(n):
        land(n, 0)
        launch(n + 1, 0)
        land(n, 1)
        launch(n + 1, 1)

    launch(0, 0)
    out_t = pltpu.make_async_copy(gt, gt_ref, local_sem.at[0])
    out_t.start()
    land(0, 0)
    launch(1, 0)
    launch(0, 1)
    land(1, 0)
    launch(2, 0)
    land(0, 1)
    launch(1, 1)
    land(2, 0)
    launch(3, 0)
    land(1, 1)
    launch(2, 1)
    land(3, 0)
    launch(4, 0)
    land(2, 1)
    launch(3, 1)
    xg.start_cross(2, 2)
    xg.pass_own()
    xg.pass_cross(0)
    xg.pass_cross(1)
    land(4, 0)
    launch(5, 0)
    land(3, 1)
    launch(4, 1)
    land(5, 0)

    def tile(m, n, k, count):
        block = full[m, n, k // 4, pl.ds(k % 4, count)]
        return block.astype(F32).reshape(64 * count, 128)

    def scales(k, carry):
        rows = pl.ds(pl.multiple_of(k * 64, 64), 64)
        block = tile(0, k, k, 1)
        diagonal = jnp.where(eye, block + pltpu.roll(block, 64, 1), 0.0)
        dcol[rows, :] = jnp.broadcast_to(lax.rsqrt(jnp.sum(diagonal, axis=1, keepdims=True)), (64, 128))
        across = jnp.sum(diagonal, axis=0, keepdims=True)
        across = lax.rsqrt(across + pltpu.roll(across, 64, 1))
        drow[:, pl.ds(pl.multiple_of(k * 128, 128), 128)] = jnp.broadcast_to(across, (8, 128))
        return carry

    lax.fori_loop(0, 8, scales, 0, unroll=True)

    def scaled_rows(m, k, factor, out, left_out, right_out):
        rows = pl.ds(pl.multiple_of(k * 64, 64), 64)
        top, bottom = pl.ds(pl.multiple_of(k * 128, 128), 64), pl.ds(pl.multiple_of(k * 128 + 64, 64), 64)
        left = dcol[rows, :] * (0.5 * factor)
        for n in range(0, 8, 2):
            turned = tile(m, k, n, 2).T
            re, im = turned[0:64], -turned[64:128]
            back = (
                jnp.where(lane64, re, pltpu.roll(im, 64, 1)),
                jnp.where(lane64, pltpu.roll(re, 64, 1), im),
            )
            for i in range(2):
                lanes = pl.ds(128 * (n + i), 128)
                right = drow[0:1, lanes]
                block = tile(m, n + i, k, 1)
                value = (block + back[i]) * left * right
                if m == 0:
                    value = jnp.where((eye | eye_im) & (k == n + i), 0.0, value)
                    left_out[rows, lanes] = value.astype(BF16)
                else:
                    exact = (block + pltpu.roll(block, 64, 1)) * 2.0 * left * right
                    value = jnp.where(eye & (k == n + i), exact, value)
                    value = jnp.where(eye_im & (k == n + i), 0.0, value)
                out[rows, lanes] = value
                right_out[top, lanes] = value.astype(BF16)
                right_out[bottom, lanes] = times_i(value).astype(BF16)

    def put_right(right, lanes, value):
        turned = times_i(value)
        for k in range(8):
            rows = slice(64 * k, 64 * k + 64)
            right[pl.ds(128 * k, 64), lanes] = value[rows].astype(BF16)
            right[pl.ds(128 * k + 64, 64), lanes] = turned[rows].astype(BF16)

    def by_columns(body, init=0):
        def column_block(n, carry):
            return body(n, pl.ds(pl.multiple_of(n * 256, 256), 256), carry)

        return lax.fori_loop(0, 4, column_block, init, unroll=True)

    def column_sum(value):
        return jnp.sum(value, axis=0, keepdims=True)

    zero_row = jnp.zeros((1, 256), F32)

    def margin_rows(k, carry):
        scaled_rows(0, k, -1.0, one, left_a, right_a)
        return carry

    lax.fori_loop(0, 8, margin_rows, 0)
    xg.pass_cross(2)
    land(4, 1)
    launch(5, 1)

    def second_power(n, lanes, carry):
        value = dot(left_a[...], right_a[:, lanes])
        two[:, lanes] = value
        put_right(right_b, lanes, value + one[:, lanes])
        return carry

    by_columns(second_power)
    xg.pass_cross(3)
    xg.pass_last(0)
    land(5, 1)

    def third_power(n, lanes, carry):
        value = dot(left_a[...], right_b[:, lanes])
        cube = value - two[:, lanes]
        left_b[:, lanes] = cube.astype(BF16)
        one[:, lanes] = one[:, lanes] + value
        scaled_rows(1, 2 * n, 1.0, four, None, right_c)
        scaled_rows(1, 2 * n + 1, 1.0, four, None, right_c)
        return carry + column_sum(cube * cube)

    cube_norm = by_columns(third_power, zero_row)
    xg.pass_last(1)

    def series(n, lanes, carry):
        value = one[:, lanes] + dot(left_b[...], right_b[:, lanes])
        two[:, lanes] = value
        left_a[:, lanes] = value.astype(BF16)
        put_right(right_a, lanes, value)
        return carry

    by_columns(series)
    xg.pass_last(2)
    xg.pass_last(3)

    def first_product(n, lanes, carry):
        value = four[:, lanes] + dot(left_a[...], right_c[:, lanes])
        one[:, lanes] = value
        left_b[:, lanes] = value.astype(BF16)
        return carry

    by_columns(first_product)

    def second_product(n, lanes, carry):
        value = one[:, lanes] + dot(left_b[...], right_a[:, lanes])
        three[:, lanes] = value
        put_right(right_b, lanes, value)
        return (carry[0] + column_sum(value * four[:, lanes]), carry[1] + column_sum(value * one[:, lanes]))

    sums = by_columns(second_product, (zero_row, zero_row))
    trace_qh = jnp.sum(sums[0], keepdims=True)
    trace_pq = jnp.sum(sums[1], keepdims=True)
    rs = lax.rsqrt(jnp.maximum(trace_qh, 0.0) * (1.0 / 512) + 1e-6)
    own = pl.ds(pl.multiple_of(b * 64, 64), 64)
    own_lanes = pl.ds(pl.multiple_of(b * 128, 128), 128)
    product = dot(left_b[own, :], right_b[...])
    four[own, :] = two[own, :] - three[own, :] * rs + product * (0.25 * rs * rs)
    four[own, own_lanes] = four[own, own_lanes] + jnp.where(eye, 1.0, 0.0)
    left = jnp.concatenate([dcol[own, :]] * 8, axis=1)
    z_ref[...] = rotation_weights(rounded(four[own, :] * left * drow[0:1, :]))

    def trace_of(ref):
        total = jnp.zeros((64, 128), F32)
        for k in range(8):
            total = total + jnp.where(eye, ref[pl.ds(k * 64, 64), pl.ds(k * 128, 128)], 0.0)
        return jnp.sum(total, keepdims=True)

    trace_w = 512.0 + trace_of(two)
    trace_z = trace_w - trace_of(three) * rs + trace_pq * (0.25 * rs * rs)
    small = jnp.sum(cube_norm, keepdims=True) < 0.0225
    ok = small & (trace_z > 0.6 * trace_w)
    ok_ref[...] = jnp.broadcast_to(jnp.where(ok, 1, 0).astype(jnp.int32), (8, 128))

    xg.finish()
    tg.drain()
    xg.drain()
    own_x.wait()
    out_t.wait()


def fast_filter(trial, applied, extra, scale):
    vmem = pl.BlockSpec(memory_space=pltpu.VMEM)
    anywhere = pl.BlockSpec(memory_space=pl.ANY)
    sem = pltpu.SemaphoreType.DMA
    square = pltpu.VMEM((512, 1024), F32)
    left = pltpu.VMEM((512, 1024), BF16)
    right = pltpu.VMEM((1024, 1024), BF16)
    return pl.pallas_call(
        functools.partial(fast_kernel, scale),
        out_shape=(
            jax.ShapeDtypeStruct((8, 128, 1024), BF16),
            jax.ShapeDtypeStruct((8, 256, 1024), BF16),
            jax.ShapeDtypeStruct((128, 1024), BF16),
            jax.ShapeDtypeStruct((8, 128), jnp.int32),
        ),
        in_specs=[vmem] * 3,
        out_specs=(anywhere, anywhere, vmem, vmem),
        scratch_shapes=[
            pltpu.VMEM((128, 1024), BF16),
            pltpu.VMEM((256, 1024), BF16),
            pltpu.VMEM((8, 128, 1024), BF16),
            pltpu.VMEM((2, 8, 64, 128), F32),
            pltpu.VMEM((2, 4, 64, 128), F32),
            pltpu.VMEM((2, 4, 64, 128), F32),
            pltpu.VMEM((2, 3, 64, 128), F32),
            pltpu.VMEM((2, 2, 4, 64, 128), BF16),
            pltpu.VMEM((2, 8, 2, 4, 64, 128), BF16),
            pltpu.VMEM((512, 128), F32),
            pltpu.VMEM((8, 1024), F32),
            left,
            left,
            right,
            right,
            right,
            square,
            square,
            square,
            square,
            sem((20,)),
            sem((20,)),
            sem((20,)),
            sem((20,)),
            sem((2, 18)),
            sem((2, 18)),
            sem((2,)),
        ],
        compiler_params=pltpu.CompilerParams(
            collective_id=1, has_side_effects=True, vmem_limit_bytes=48 * 2**20
        ),
    )(trial, applied, extra)


def rotation_weights(z):
    turned = times_i(z)
    re_part = jnp.where(iota((64, 1024), 1) % 128 < 64, z, -z)
    im_part = jnp.where(iota((64, 1024), 1) % 128 < 64, -turned, turned)
    both = jnp.concatenate([re_part, im_part], axis=0).astype(BF16)
    return dot(unweave(False), both).astype(BF16)


def turn_blocks(weights, gt, gx, outs):
    width = gt.shape[2]
    sources = (gt[...], gx[:, 0:128, :], gx[:, 128:256, :])
    for out, source in zip(outs, sources):
        value = dot(weights, source.reshape(1024, width)).astype(BF16)
        out[...] = value.reshape(64, 2, width)


def fast_rotate_kernel(z_ref, gt, gx, *outs):
    turn_blocks(z_ref[...], gt, gx, outs)


def fast_rotate(z, gt, gx):
    width = 256
    return pl.pallas_call(
        fast_rotate_kernel,
        grid=(1024 // width,),
        out_shape=(jax.ShapeDtypeStruct((64, 2, 1024), BF16),) * 3,
        in_specs=[
            pl.BlockSpec((128, 1024), lambda n: (0, 0)),
            pl.BlockSpec((8, 128, width), lambda n: (0, 0, n)),
            pl.BlockSpec((8, 256, width), lambda n: (0, 0, n)),
        ],
        out_specs=(pl.BlockSpec((64, 2, width), lambda n: (0, 0, n)),) * 3,
        compiler_params=pltpu.CompilerParams(vmem_limit_bytes=48 * 2**20),
    )(z, gt, gx)


def rotate_kernel(full, gt, gx, o_ref, o_next, o_last, w, ham, p, q, pq, high, low):
    b = lax.axis_index("band")
    own = pl.ds(pl.multiple_of(b * 64, 64), 64)
    hermitian_part(full, 0, w)
    hermitian_part(full, 1, ham)
    invert(w)
    expand(ham, high, low)
    product(w, pl.ds(0, 512), high, low, p)
    expand(w, high, low)
    product(p, pl.ds(0, 512), high, low, q)
    total = jnp.sum(q[...] * ham[...], keepdims=True)
    rs = lax.rsqrt(jnp.maximum(total, 0.0) * (1.0 / 512) + 1e-6)
    expand(q, high, low)
    product(p, own, high, low, pq)
    z = w[own, :] - q[own, :] * rs + pq[...] * (0.25 * rs * rs)
    turn_blocks(rotation_weights(z.astype(BF16).astype(F32)), gt, gx, (o_ref, o_next, o_last))


def rotate(full, gt, gx):
    vmem = pl.BlockSpec(memory_space=pltpu.VMEM)
    return pl.pallas_call(
        rotate_kernel,
        out_shape=(jax.ShapeDtypeStruct((64, 2, 1024), BF16),) * 3,
        in_specs=[vmem] * 3,
        out_specs=(vmem,) * 3,
        scratch_shapes=[
            pltpu.VMEM((512, 1024), F32),
            pltpu.VMEM((512, 1024), F32),
            pltpu.VMEM((512, 1024), F32),
            pltpu.VMEM((512, 1024), F32),
            pltpu.VMEM((64, 1024), F32),
            pltpu.VMEM((1024, 1024), BF16),
            pltpu.VMEM((1024, 1024), BF16),
        ],
        compiler_params=pltpu.CompilerParams(vmem_limit_bytes=48 * 2**20),
    )(full, gt, gx)


def local(trial, applied, extra):
    rows, _, length = trial.shape
    scale = 1.0 / (length * lax.axis_size("ga"))
    gt, gx, z, ok = fast_filter(trial, applied, extra, scale)

    def planes(block):
        return jnp.swapaxes(block, 0, 1).reshape(2 * rows, length)

    def direct():
        margin = (trial.astype(F32) + extra.astype(F32)).astype(BF16)
        rest = jnp.concatenate([planes(applied), planes(margin)], axis=0)
        blocks, others, full = exchange(planes(trial), rest, scale)
        return tuple(rotate(full.reshape(2, 8, 512, 128), blocks, others))

    return lax.cond(ok[0, 0] > 0, lambda: tuple(fast_rotate(z, gt, gx)), direct)


def solution(mesh):
    spec = P("band", None, "ga")
    return jax.shard_map(local, mesh=mesh, in_specs=(spec,) * 3, out_specs=(spec,) * 3, check_vma=False)
```

```python
import functools

import jax
import jax.numpy as jnp
from jax import lax
from jax.experimental import pallas as pl
from jax.experimental.pallas import tpu as pltpu
from jax.sharding import PartitionSpec as P

MESH = pl.DeviceIdType.MESH
F32 = jnp.float32
BF16 = jnp.bfloat16


def iota(shape, dim):
    return lax.broadcasted_iota(jnp.int32, shape, dim)


def remote(src, dst, send_sem, recv_sem, device):
    return pltpu.make_async_remote_copy(
        src_ref=src,
        dst_ref=dst,
        send_sem=send_sem,
        recv_sem=recv_sem,
        device_id=device,
        device_id_type=MESH,
    )


def exchange_kernel(scale, t_ref, x_ref, gt_ref, gx_ref, full_ref, gt, part, core_in, mid, x_in, low, z_in, full,
                    t_send, t_recv, x_send, x_recv, s_send, s_recv, local_sem):
    g = lax.axis_index("ga")
    b = lax.axis_index("band")
    zl, x, c = g // 8, (g // 2) % 4, g % 2
    h, y = b // 4, b % 4
    partner = (1 - h) * 4 + y
    y_up, y_dn, y_far = (y + 1) % 4, (y + 3) % 4, (y + 2) % 4

    def band_at(hh, yy):
        return hh * 4 + yy

    def ga_at(zz, xx, cc):
        return zz * 8 + xx * 2 + cc

    barrier = pltpu.get_barrier_semaphore()
    greet = [(g, (b + d) % 8) for d in range(1, 8)]
    greet += [(ga_at(zl, x, 1 - c), b)]
    greet += [(ga_at(zl, (x + d) % 4, c), b) for d in range(1, 4)]
    greet += [(ga_at((zl + d) % 4, x, c), b) for d in range(1, 4)]
    for device in greet:
        pl.semaphore_signal(barrier, inc=1, device_id=device, device_id_type=MESH)
    pl.semaphore_wait(barrier, len(greet))

    up, dn, over = (g, band_at(h, y_up)), (g, band_at(h, y_dn)), (g, partner)

    def gather(own, slots, half, send, recv):
        def move(n, src, block, rows, device):
            return remote(src, slots.at[block, rows], send.at[n], recv.at[n], device)

        whole = pl.ds(0, 2 * half)
        lo, hi = pl.ds(0, half), pl.ds(half, half)
        b_dn, b_up = band_at(h, y_dn), band_at(h, y_up)
        p_dn, p_up = band_at(1 - h, y_dn), band_at(1 - h, y_up)
        first = [move(0, own, b, whole, over), move(1, own, b, whole, up), move(2, own, b, whole, dn)]
        second = [
            move(3, slots.at[partner], partner, whole, up),
            move(4, slots.at[partner], partner, whole, dn),
            move(5, slots.at[b_dn, lo], b_dn, lo, up),
            move(6, slots.at[b_up, hi], b_up, hi, dn),
            move(7, slots.at[p_dn, lo], p_dn, lo, up),
            move(8, slots.at[p_up, hi], p_up, hi, dn),
        ]

        def start():
            for copy in first:
                copy.start()

        def forward_own():
            first[1].wait_recv()
            second[2].start()
            first[2].wait_recv()
            second[3].start()

        def forward_partner():
            first[0].wait_recv()
            second[0].start()
            second[1].start()

        def forward_far():
            second[0].wait_recv()
            second[4].start()
            second[1].wait_recv()
            second[5].start()

        def finish():
            for copy in second[2:]:
                copy.wait_recv()

        def drain():
            for copy in first + second:
                copy.wait_send()

        return start, forward_own, forward_partner, forward_far, finish, drain

    t_start, t_own, t_partner, t_far, t_finish, t_drain = gather(t_ref, gt, 64, t_send, t_recv)
    x_start, x_own, x_partner, x_far, x_finish, x_drain = gather(x_ref, gx_ref, 128, x_send, x_recv)
    t_start()
    own_t = pltpu.make_async_copy(t_ref, gt.at[b], local_sem.at[0])
    own_t.start()
    own_x = pltpu.make_async_copy(x_ref, gx_ref.at[b], local_sem.at[1])
    own_x.start()
    own_t.wait()
    own_x.wait()
    t_own()
    t_partner()
    t_far()
    t_finish()
    t_drain()
    x_start()

    sign = jnp.where(iota((64, 128), 1) < 64, scale, -scale).astype(F32)

    def gram(k, carry):
        u = lax.dot_general(
            x_ref[...], gt[k], (((1,), (1,)), ((), ())), preferred_element_type=F32
        )
        part[1, k] = u[0:64] * sign + pltpu.roll(u[64:128], 64, 1) * scale
        part[0, k] = u[128:192] * sign + pltpu.roll(u[192:256], 64, 1) * scale
        return carry

    lax.fori_loop(0, 8, gram, 0)

    sib = (ga_at(zl, x, 1 - c), b)
    move = remote(part.at[:, pl.ds((1 - c) * 4, 4)], core_in, s_send.at[0], s_recv.at[0], sib)
    move.start()
    move.wait()
    mid[...] = part[:, pl.ds(c * 4, 4)] + core_in[...]

    moves = [
        remote(mid.at[:, (x + d) % 4], x_in.at[d - 1], s_send.at[d], s_recv.at[d], (ga_at(zl, (x + d) % 4, c), b))
        for d in range(1, 4)
    ]
    for move in moves:
        move.start()
    for move in moves:
        move.wait()
    low[...] = mid[:, x] + x_in[0] + x_in[1] + x_in[2]

    moves = [
        remote(
            low.at[:, pl.ds(((zl + d) % 4) * 16, 16)],
            z_in.at[d - 1],
            s_send.at[3 + d],
            s_recv.at[3 + d],
            (ga_at((zl + d) % 4, x, c), b),
        )
        for d in range(1, 4)
    ]
    for move in moves:
        move.start()
    for move in moves:
        move.wait()
    blk = c * 4 + x
    full[:, blk, b, zl] = low[:, pl.ds(zl * 16, 16)] + z_in[0] + z_in[1] + z_in[2]

    x_own()
    x_partner()

    def spread(view, base, devices):
        moves = [
            remote(view, view, s_send.at[base + n], s_recv.at[base + n], device) for n, device in enumerate(devices)
        ]
        for move in moves:
            move.start()
        for move in moves:
            move.wait()

    spread(full.at[:, blk, b, zl], 7, [(g, (b + d) % 8) for d in range(1, 8)])
    spread(full.at[:, blk, :, zl], 14, [(ga_at((zl + d) % 4, x, c), b) for d in range(1, 4)])
    spread(full.at[:, blk], 17, [(ga_at(zl, (x + d) % 4, c), b) for d in range(1, 4)])
    spread(full.at[:, pl.ds(c * 4, 4)], 20, [sib])

    out_t = pltpu.make_async_copy(gt, gt_ref, local_sem.at[0])
    out_f = pltpu.make_async_copy(full, full_ref, local_sem.at[1])
    out_t.start()
    out_f.start()
    x_far()
    x_finish()
    x_drain()
    out_t.wait()
    out_f.wait()


def exchange(trial, rest, scale):
    vmem = pl.BlockSpec(memory_space=pltpu.VMEM)
    anywhere = pl.BlockSpec(memory_space=pl.ANY)
    sem = pltpu.SemaphoreType.DMA
    return pl.pallas_call(
        functools.partial(exchange_kernel, scale),
        out_shape=(
            jax.ShapeDtypeStruct((8, 128, 1024), BF16),
            jax.ShapeDtypeStruct((8, 256, 1024), BF16),
            jax.ShapeDtypeStruct((2, 8, 8, 4, 16, 128), F32),
        ),
        in_specs=[vmem, vmem],
        out_specs=(anywhere, anywhere, anywhere),
        scratch_shapes=[
            pltpu.VMEM((8, 128, 1024), BF16),
            pltpu.VMEM((2, 8, 64, 128), F32),
            pltpu.VMEM((2, 4, 64, 128), F32),
            pltpu.VMEM((2, 4, 64, 128), F32),
            pltpu.VMEM((3, 2, 64, 128), F32),
            pltpu.VMEM((2, 64, 128), F32),
            pltpu.VMEM((3, 2, 16, 128), F32),
            pltpu.VMEM((2, 8, 8, 4, 16, 128), F32),
            sem((9,)),
            sem((9,)),
            sem((9,)),
            sem((9,)),
            sem((21,)),
            sem((21,)),
            sem((2,)),
        ],
        compiler_params=pltpu.CompilerParams(
            collective_id=0, has_side_effects=True, vmem_limit_bytes=48 * 2**20
        ),
    )(trial, rest)


def invert_pivot(block):
    lane, row = iota((64, 128), 1), iota((64, 128), 0)
    one = lane[:1]
    for k in range(0, 64, 2):
        m = k + 1
        c0r = jnp.broadcast_to(block[:, k : k + 1], (64, 128))
        c0i = jnp.broadcast_to(block[:, 64 + k : 65 + k], (64, 128))
        c1r = jnp.broadcast_to(block[:, m : m + 1], (64, 128))
        c1i = jnp.broadcast_to(block[:, 64 + m : 65 + m], (64, 128))
        r0, r1 = block[k : k + 1, :], block[m : m + 1, :]
        s0, s1 = pltpu.roll(r0, 64, 1), pltpu.roll(r1, 64, 1)
        s0, s1 = jnp.where(one < 64, -s0, s0), jnp.where(one < 64, -s1, s1)
        a, br, bi, c = c0r[k : k + 1], c1r[k : k + 1], c1i[k : k + 1], c1r[m : m + 1]
        e0, e0i, e1, e1i = one == k, one == 64 + k, one == m, one == 64 + m
        r0 = jnp.where(e0, 1.0, jnp.where(e0i | e1 | e1i, 0.0, r0))
        s0 = jnp.where(e0i, 1.0, jnp.where(e0 | e1 | e1i, 0.0, s0))
        r1 = jnp.where(e1, 1.0, jnp.where(e1i | e0 | e0i, 0.0, r1))
        s1 = jnp.where(e1i, 1.0, jnp.where(e1 | e0 | e0i, 0.0, s1))
        ra = 1.0 / a
        tr, ti = br * ra, bi * ra
        rs = 1.0 / (c - (br * br + bi * bi) * ra)
        i01r, i01i = -tr * rs, -ti * rs
        i00 = ra + (tr * tr + ti * ti) * rs
        q0 = i00 * r0 + i01r * r1 + i01i * s1
        q1 = i01r * r0 - i01i * s0 + rs * r1
        u0 = i00 * s0 + i01r * s1 - i01i * r1
        u1 = i01r * s0 + i01i * r0 + rs * s1
        isk, ism = row == k, row == m
        c0r = jnp.where(isk, -1.0, jnp.where(ism, 0.0, c0r))
        c1r = jnp.where(ism, -1.0, jnp.where(isk, 0.0, c1r))
        c0i, c1i = jnp.where(isk | ism, 0.0, c0i), jnp.where(isk | ism, 0.0, c1i)
        dead = isk | ism | (lane == k) | (lane == m) | (lane == 64 + k) | (lane == 64 + m)
        block = jnp.where(dead, 0.0, block) - c0r * q0 - c0i * u0 - c1r * q1 - c1i * u1
    return block


def halves(value):
    high = value.astype(BF16)
    return high, (value - high.astype(F32)).astype(BF16)


def dot(a, b):
    return jnp.dot(a, b, preferred_element_type=F32)


def dot_split(a, b):
    ah, al = halves(a)
    bh, bl = halves(b)
    return dot(ah, bh) + dot(al, bh) + dot(ah, bl)


def times_i(value):
    tiles = [pltpu.roll(value[:, n : n + 128], 64, 1) for n in range(0, value.shape[1], 128)]
    turned = jnp.concatenate(tiles, axis=1)
    return jnp.where(iota(value.shape, 1) % 128 < 64, -turned, turned)


def invert(work):
    def step(k, carry):
        rows, lanes = pl.ds(pl.multiple_of(k * 64, 64), 64), pl.ds(pl.multiple_of(k * 128, 128), 128)
        pivot = invert_pivot(work[rows, lanes])
        panel = work[rows, :]
        panel = dot_split(pivot, jnp.concatenate([panel, times_i(panel)], axis=0))
        panel = jnp.where(iota((64, 1024), 1) // 128 == k, jnp.concatenate([pivot] * 8, axis=1), panel)
        column = jnp.where(iota((512, 128), 0) // 64 == k, 0.0, work[:, lanes])
        work[:, lanes] = jnp.zeros((512, 128), F32)
        work[...] = work[...] - dot_split(column, jnp.concatenate([panel, times_i(panel)], axis=0))
        work[rows, :] = panel
        return carry

    lax.fori_loop(0, 8, step, 0)


def hermitian_part(full, m, out):
    lane = iota((64, 128), 1) < 64

    def row_block(k, carry):
        rows = pl.ds(pl.multiple_of(k * 64, 64), 64)
        for n in range(0, 8, 2):
            turned = full[m, k, pl.ds(64 * n, 128), :].T
            re, im = turned[0:64], -turned[64:128]
            left = jnp.where(lane, re, pltpu.roll(im, 64, 1))
            right = jnp.where(lane, pltpu.roll(re, 64, 1), im)
            out[rows, pl.ds(128 * n, 128)] = (full[m, n, rows, :] + left) * 0.5
            out[rows, pl.ds(128 * n + 128, 128)] = (full[m, n + 1, rows, :] + right) * 0.5
        return carry

    lax.fori_loop(0, 8, row_block, 0)


def expand(value_ref, high, low):
    def row_block(k, carry):
        rows = pl.ds(pl.multiple_of(k * 64, 64), 64)
        value = value_ref[rows, :]
        vh, vl = halves(value)
        th, tl = halves(times_i(value))
        top, bottom = pl.ds(pl.multiple_of(k * 128, 128), 64), pl.ds(pl.multiple_of(k * 128 + 64, 64), 64)
        high[top, :], high[bottom, :], low[top, :], low[bottom, :] = vh, th, vl, tl
        return carry

    lax.fori_loop(0, 8, row_block, 0)


def product(left_ref, rows, high, low, out):
    def column_block(n, carry):
        lanes = pl.ds(pl.multiple_of(n * 256, 256), 256)
        ah, al = halves(left_ref[rows, :])
        bh = high[:, lanes]
        out[:, lanes] = dot(ah, bh) + dot(al, bh) + dot(ah, low[:, lanes])
        return carry

    lax.fori_loop(0, 4, column_block, 0)


def unweave(to_planes):
    row, col = iota((128, 128), 0), iota((128, 128), 1)
    if not to_planes:
        row, col = col, row
    source = jnp.where(row < 64, 2 * row, 2 * row - 127)
    return jnp.where(col == source, 1.0, 0.0).astype(BF16)


def fast_kernel(scale, trial, applied, extra, gt_ref, gx_ref, z_ref, ok_ref, t_ref, x_ref, gt, part, core_in, mid, x_in,
                ring, full, dcol, drow, left_a, left_b, right_a, right_b, right_c, one, two, three, four, t_send,
                t_recv, x_send, x_recv, s_send, s_recv, local_sem):
    g = lax.axis_index("ga")
    b = lax.axis_index("band")
    zl, x, c = g // 8, (g // 2) % 4, g % 2
    h, y = b // 4, b % 4
    partner = (1 - h) * 4 + y
    y_up, y_dn, y_far = (y + 1) % 4, (y + 3) % 4, (y + 2) % 4

    def band_at(hh, yy):
        return hh * 4 + yy

    def ga_at(zz, xx, cc):
        return zz * 8 + xx * 2 + cc

    def ring_at(d):
        z = (h * 4 + zl + d) % 8
        return (ga_at(z % 4, x, c), band_at(z // 4, y))

    sib = (ga_at(zl, x, 1 - c), b)
    xs = [(ga_at(zl, (x + d) % 4, c), b) for d in range(1, 4)]
    ys = [(g, band_at(h, (y + d) % 4)) for d in range(1, 4)]
    rings = [ring_at(d) for d in range(1, 8)]
    barrier = pltpu.get_barrier_semaphore()
    greet = [sib] + xs + ys + rings
    for device in greet:
        pl.semaphore_signal(barrier, inc=1, device_id=device, device_id_type=MESH)
    planes = unweave(True)
    t_ref[...] = dot(planes, trial[...].reshape(128, 1024)).astype(BF16)
    pl.semaphore_wait(barrier, len(greet))

    up, dn, over = (g, band_at(h, y_up)), (g, band_at(h, y_dn)), (g, partner)
    b_dn, b_up, b_far = band_at(h, y_dn), band_at(h, y_up), band_at(h, y_far)
    p_dn, p_up, p_far = band_at(1 - h, y_dn), band_at(1 - h, y_up), band_at(1 - h, y_far)

    class Gather:
        def __init__(self, own, slots, size, send, recv):
            def move(n, src, block, rows, device):
                return remote(src, slots.at[block, rows], send.at[n], recv.at[n], device)

            def relay(n, block, rows, device):
                return move(n, slots.at[block, rows], block, rows, device)

            step = size // 4
            piece = [pl.ds(n * step, step) for n in range(4)]
            whole, lo, hi = pl.ds(0, size), pl.ds(0, size // 2), pl.ds(size // 2, size // 2)
            self.cross = [move(n, own.at[piece[n]], b, piece[n], over) for n in range(4)]
            self.near = [move(4, own, b, whole, up), move(5, own, b, whole, dn)]
            self.far = [relay(6, b_dn, lo, up), relay(7, b_up, hi, dn)]
            self.to_up = [relay(8 + n, partner, piece[n], up) for n in range(4)]
            self.to_dn = [relay(12 + n, partner, piece[n], dn) for n in range(4)]
            self.last = [relay(16, p_dn, piece[0], up), relay(17, p_dn, piece[1], up)]
            self.last += [relay(18, p_up, piece[2], dn), relay(19, p_up, piece[3], dn)]

        def start_near(self):
            for copy in self.near:
                copy.start()

        def start_cross(self, first, count):
            for copy in self.cross[first : first + count]:
                copy.start()

        def pass_own(self):
            for n in range(2):
                self.near[n].wait_recv()
                self.far[n].start()

        def pass_cross(self, n):
            self.cross[n].wait_recv()
            self.to_up[n].start()
            self.to_dn[n].start()

        def pass_last(self, n):
            (self.to_up if n < 2 else self.to_dn)[n].wait_recv()
            self.last[n].start()

        def finish(self):
            for copy in self.far + self.to_up[2:] + self.to_dn[:2] + self.last:
                copy.wait_recv()

        def drain(self):
            for copy in self.cross + self.near + self.far + self.to_up + self.to_dn + self.last:
                copy.wait_send()

    tg = Gather(t_ref, gt, 128, t_send, t_recv)
    xg = Gather(x_ref, gx_ref, 256, x_send, x_recv)

    sign = jnp.where(iota((64, 128), 1) < 64, scale, -scale).astype(F32)

    def gram(k, block):
        u = lax.dot_general(x_ref[...], block, (((1,), (1,)), ((), ())), preferred_element_type=F32)
        part[1, k] = u[0:64] * sign + pltpu.roll(u[64:128], 64, 1) * scale
        part[0, k] = u[128:192] * sign + pltpu.roll(u[192:256], 64, 1) * scale

    tg.start_cross(0, 1)
    tg.start_near()
    tg.start_cross(1, 3)
    x_ref[0:128] = dot(planes, applied[...].reshape(128, 1024)).astype(BF16)
    margin = (trial[...].astype(F32) + extra[...].astype(F32)).astype(BF16)
    x_ref[128:256] = dot(planes, margin.reshape(128, 1024)).astype(BF16)
    own_x = pltpu.make_async_copy(x_ref, gx_ref.at[b], local_sem.at[1])
    own_x.start()
    gt[b] = t_ref[...]
    gram(b, t_ref[...])
    tg.pass_cross(0)
    tg.pass_own()
    tg.pass_cross(1)
    tg.pass_last(0)
    tg.pass_cross(2)
    tg.pass_last(1)
    tg.pass_cross(3)
    xg.start_cross(0, 2)
    gram(b_dn, gt[b_dn])
    gram(b_up, gt[b_up])
    gram(partner, gt[partner])
    tg.pass_last(2)
    tg.pass_last(3)
    tg.finish()
    xg.start_near()
    xg.start_cross(2, 2)
    for k in (b_far, p_dn, p_up, p_far):
        gram(k, gt[k])

    blk = c * 4 + x
    lane64 = iota((64, 128), 1) < 64
    eye = iota((64, 128), 0) == iota((64, 128), 1)
    eye_im = iota((64, 128), 0) + 64 == iota((64, 128), 1)

    def rounded(value):
        return value.astype(BF16).astype(F32)

    def core_moves(m):
        return [remote(part.at[m, pl.ds((1 - c) * 4, 4)], core_in.at[m], s_send.at[m, 0], s_recv.at[m, 0], sib)]

    def core_add(m):
        mid[m] = part[m, pl.ds(c * 4, 4)] + core_in[m]

    def x_moves(m):
        return [
            remote(mid.at[m, (x + d) % 4], x_in.at[m, d - 1], s_send.at[m, d], s_recv.at[m, d], xs[d - 1])
            for d in range(1, 4)
        ]

    def x_add(m):
        value = mid[m, x] + x_in[m, 0] + x_in[m, 1] + x_in[m, 2]
        turned = pltpu.roll(value, 64, 1)
        ring[m, h, zl] = jnp.where(eye_im & (blk == b), turned - rounded(turned), value).astype(BF16)

    def spread(m, view, base, devices):
        return [
            remote(view, view, s_send.at[m, base + n], s_recv.at[m, base + n], device)
            for n, device in enumerate(devices)
        ]

    def ring_add(m):
        for hh in range(2):
            value = ring[m, hh, 0].astype(F32)
            for n in range(1, 4):
                value = value + ring[m, hh, n].astype(F32)
            exact = value + pltpu.roll(value, 64, 1)
            mine = blk == hh * 4 + y
            value = jnp.where(eye & mine, exact, jnp.where(eye_im & mine, exact - rounded(exact), value))
            full[m, blk, hh, y] = value.astype(BF16)

    stages = [
        (core_moves, core_add),
        (x_moves, x_add),
        (lambda m: spread(m, ring.at[m, h, zl], 4, rings), ring_add),
        (lambda m: spread(m, full.at[m, blk, :, y], 11, ys), None),
        (lambda m: spread(m, full.at[m, blk], 14, xs), None),
        (lambda m: spread(m, full.at[m, pl.ds(c * 4, 4)], 17, [sib]), None),
    ]
    flight = {}

    def launch(n, m):
        flight[n, m] = stages[n][0](m)
        for move in flight[n, m]:
            move.start()

    def land(n, m):
        for move in flight[n, m]:
            move.wait()
        if stages[n][1] is not None:
            stages[n][1](m)

    def turn(n):
        land(n, 0)
        launch(n + 1, 0)
        land(n, 1)
        launch(n + 1, 1)

    launch(0, 0)
    out_t = pltpu.make_async_copy(gt, gt_ref, local_sem.at[0])
    out_t.start()
    land(0, 0)
    launch(1, 0)
    launch(0, 1)
    land(1, 0)
    launch(2, 0)
    land(0, 1)
    launch(1, 1)
    xg.pass_own()
    xg.pass_cross(0)
    xg.pass_cross(1)
    land(2, 0)
    launch(3, 0)
    land(1, 1)
    launch(2, 1)
    land(3, 0)
    launch(4, 0)
    land(2, 1)
    launch(3, 1)
    xg.pass_cross(2)
    xg.pass_cross(3)
    xg.pass_last(0)
    xg.pass_last(1)
    land(4, 0)
    launch(5, 0)
    land(3, 1)
    launch(4, 1)
    xg.pass_last(2)
    xg.pass_last(3)
    land(5, 0)

    def tile(m, n, k, count):
        block = full[m, n, k // 4, pl.ds(k % 4, count)]
        return block.astype(F32).reshape(64 * count, 128)

    def scales(k, carry):
        rows = pl.ds(pl.multiple_of(k * 64, 64), 64)
        block = tile(0, k, k, 1)
        diagonal = jnp.where(eye, block + pltpu.roll(block, 64, 1), 0.0)
        dcol[rows, :] = jnp.broadcast_to(lax.rsqrt(jnp.sum(diagonal, axis=1, keepdims=True)), (64, 128))
        across = jnp.sum(diagonal, axis=0, keepdims=True)
        across = lax.rsqrt(across + pltpu.roll(across, 64, 1))
        drow[:, pl.ds(pl.multiple_of(k * 128, 128), 128)] = jnp.broadcast_to(across, (8, 128))
        return carry

    lax.fori_loop(0, 8, scales, 0, unroll=True)

    def scaled_rows(m, k, factor, out, left_out, right_out):
        rows = pl.ds(pl.multiple_of(k * 64, 64), 64)
        top, bottom = pl.ds(pl.multiple_of(k * 128, 128), 64), pl.ds(pl.multiple_of(k * 128 + 64, 64), 64)
        left = dcol[rows, :] * (0.5 * factor)
        for n in range(0, 8, 2):
            turned = tile(m, k, n, 2).T
            re, im = turned[0:64], -turned[64:128]
            back = (
                jnp.where(lane64, re, pltpu.roll(im, 64, 1)),
                jnp.where(lane64, pltpu.roll(re, 64, 1), im),
            )
            for i in range(2):
                lanes = pl.ds(128 * (n + i), 128)
                right = drow[0:1, lanes]
                block = tile(m, n + i, k, 1)
                value = (block + back[i]) * left * right
                if m == 0:
                    value = jnp.where((eye | eye_im) & (k == n + i), 0.0, value)
                    left_out[rows, lanes] = value.astype(BF16)
                else:
                    exact = (block + pltpu.roll(block, 64, 1)) * 2.0 * left * right
                    value = jnp.where(eye & (k == n + i), exact, value)
                    value = jnp.where(eye_im & (k == n + i), 0.0, value)
                out[rows, lanes] = value
                right_out[top, lanes] = value.astype(BF16)
                right_out[bottom, lanes] = times_i(value).astype(BF16)

    def put_right(right, lanes, value):
        turned = times_i(value)
        for k in range(8):
            rows = slice(64 * k, 64 * k + 64)
            right[pl.ds(128 * k, 64), lanes] = value[rows].astype(BF16)
            right[pl.ds(128 * k + 64, 64), lanes] = turned[rows].astype(BF16)

    def by_columns(body, init=0):
        def column_block(n, carry):
            return body(n, pl.ds(pl.multiple_of(n * 256, 256), 256), carry)

        return lax.fori_loop(0, 4, column_block, init, unroll=True)

    def column_sum(value):
        return jnp.sum(value, axis=0, keepdims=True)

    zero_row = jnp.zeros((1, 256), F32)

    def margin_rows(k, carry):
        scaled_rows(0, k, -1.0, one, left_a, right_a)
        return carry

    lax.fori_loop(0, 8, margin_rows, 0)
    land(4, 1)
    launch(5, 1)

    def second_power(n, lanes, carry):
        value = dot(left_a[...], right_a[:, lanes])
        two[:, lanes] = value
        put_right(right_b, lanes, value + one[:, lanes])
        return carry

    by_columns(second_power)
    land(5, 1)

    def third_power(n, lanes, carry):
        value = dot(left_a[...], right_b[:, lanes])
        cube = value - two[:, lanes]
        left_b[:, lanes] = cube.astype(BF16)
        one[:, lanes] = one[:, lanes] + value
        scaled_rows(1, 2 * n, 1.0, four, None, right_c)
        scaled_rows(1, 2 * n + 1, 1.0, four, None, right_c)
        return carry + column_sum(cube * cube)

    cube_norm = by_columns(third_power, zero_row)

    def series(n, lanes, carry):
        value = one[:, lanes] + dot(left_b[...], right_b[:, lanes])
        two[:, lanes] = value
        left_a[:, lanes] = value.astype(BF16)
        put_right(right_a, lanes, value)
        return carry

    by_columns(series)

    def first_product(n, lanes, carry):
        value = four[:, lanes] + dot(left_a[...], right_c[:, lanes])
        one[:, lanes] = value
        left_b[:, lanes] = value.astype(BF16)
        return carry

    by_columns(first_product)

    def second_product(n, lanes, carry):
        value = one[:, lanes] + dot(left_b[...], right_a[:, lanes])
        three[:, lanes] = value
        put_right(right_b, lanes, value)
        return (carry[0] + column_sum(value * four[:, lanes]), carry[1] + column_sum(value * one[:, lanes]))

    sums = by_columns(second_product, (zero_row, zero_row))
    trace_qh = jnp.sum(sums[0], keepdims=True)
    trace_pq = jnp.sum(sums[1], keepdims=True)
    rs = lax.rsqrt(jnp.maximum(trace_qh, 0.0) * (1.0 / 512) + 1e-6)
    own = pl.ds(pl.multiple_of(b * 64, 64), 64)
    own_lanes = pl.ds(pl.multiple_of(b * 128, 128), 128)
    product = dot(left_b[own, :], right_b[...])
    four[own, :] = two[own, :] - three[own, :] * rs + product * (0.25 * rs * rs)
    four[own, own_lanes] = four[own, own_lanes] + jnp.where(eye, 1.0, 0.0)
    left = jnp.concatenate([dcol[own, :]] * 8, axis=1)
    z_ref[...] = rotation_weights(rounded(four[own, :] * left * drow[0:1, :]))

    def trace_of(ref):
        total = jnp.zeros((64, 128), F32)
        for k in range(8):
            total = total + jnp.where(eye, ref[pl.ds(k * 64, 64), pl.ds(k * 128, 128)], 0.0)
        return jnp.sum(total, keepdims=True)

    trace_w = 512.0 + trace_of(two)
    trace_z = trace_w - trace_of(three) * rs + trace_pq * (0.25 * rs * rs)
    small = jnp.sum(cube_norm, keepdims=True) < 0.0225
    ok = small & (trace_z > 0.6 * trace_w)
    ok_ref[...] = jnp.broadcast_to(jnp.where(ok, 1, 0).astype(jnp.int32), (8, 128))

    xg.finish()
    tg.drain()
    xg.drain()
    own_x.wait()
    out_t.wait()


def fast_filter(trial, applied, extra, scale):
    vmem = pl.BlockSpec(memory_space=pltpu.VMEM)
    anywhere = pl.BlockSpec(memory_space=pl.ANY)
    sem = pltpu.SemaphoreType.DMA
    square = pltpu.VMEM((512, 1024), F32)
    left = pltpu.VMEM((512, 1024), BF16)
    right = pltpu.VMEM((1024, 1024), BF16)
    return pl.pallas_call(
        functools.partial(fast_kernel, scale),
        out_shape=(
            jax.ShapeDtypeStruct((8, 128, 1024), BF16),
            jax.ShapeDtypeStruct((8, 256, 1024), BF16),
            jax.ShapeDtypeStruct((128, 1024), BF16),
            jax.ShapeDtypeStruct((8, 128), jnp.int32),
        ),
        in_specs=[vmem] * 3,
        out_specs=(anywhere, anywhere, vmem, vmem),
        scratch_shapes=[
            pltpu.VMEM((128, 1024), BF16),
            pltpu.VMEM((256, 1024), BF16),
            pltpu.VMEM((8, 128, 1024), BF16),
            pltpu.VMEM((2, 8, 64, 128), F32),
            pltpu.VMEM((2, 4, 64, 128), F32),
            pltpu.VMEM((2, 4, 64, 128), F32),
            pltpu.VMEM((2, 3, 64, 128), F32),
            pltpu.VMEM((2, 2, 4, 64, 128), BF16),
            pltpu.VMEM((2, 8, 2, 4, 64, 128), BF16),
            pltpu.VMEM((512, 128), F32),
            pltpu.VMEM((8, 1024), F32),
            left,
            left,
            right,
            right,
            right,
            square,
            square,
            square,
            square,
            sem((20,)),
            sem((20,)),
            sem((20,)),
            sem((20,)),
            sem((2, 18)),
            sem((2, 18)),
            sem((2,)),
        ],
        compiler_params=pltpu.CompilerParams(
            collective_id=1, has_side_effects=True, vmem_limit_bytes=48 * 2**20
        ),
    )(trial, applied, extra)


def rotation_weights(z):
    turned = times_i(z)
    re_part = jnp.where(iota((64, 1024), 1) % 128 < 64, z, -z)
    im_part = jnp.where(iota((64, 1024), 1) % 128 < 64, -turned, turned)
    both = jnp.concatenate([re_part, im_part], axis=0).astype(BF16)
    return dot(unweave(False), both).astype(BF16)


def turn_blocks(weights, gt, gx, outs):
    width = gt.shape[2]
    sources = (gt[...], gx[:, 0:128, :], gx[:, 128:256, :])
    for out, source in zip(outs, sources):
        value = dot(weights, source.reshape(1024, width)).astype(BF16)
        out[...] = value.reshape(64, 2, width)


def fast_rotate_kernel(z_ref, gt, gx, *outs):
    turn_blocks(z_ref[...], gt, gx, outs)


def fast_rotate(z, gt, gx):
    width = 512
    return pl.pallas_call(
        fast_rotate_kernel,
        grid=(1024 // width,),
        out_shape=(jax.ShapeDtypeStruct((64, 2, 1024), BF16),) * 3,
        in_specs=[
            pl.BlockSpec((128, 1024), lambda n: (0, 0)),
            pl.BlockSpec((8, 128, width), lambda n: (0, 0, n)),
            pl.BlockSpec((8, 256, width), lambda n: (0, 0, n)),
        ],
        out_specs=(pl.BlockSpec((64, 2, width), lambda n: (0, 0, n)),) * 3,
        compiler_params=pltpu.CompilerParams(vmem_limit_bytes=48 * 2**20),
    )(z, gt, gx)


def rotate_kernel(full, gt, gx, o_ref, o_next, o_last, w, ham, p, q, pq, high, low):
    b = lax.axis_index("band")
    own = pl.ds(pl.multiple_of(b * 64, 64), 64)
    hermitian_part(full, 0, w)
    hermitian_part(full, 1, ham)
    invert(w)
    expand(ham, high, low)
    product(w, pl.ds(0, 512), high, low, p)
    expand(w, high, low)
    product(p, pl.ds(0, 512), high, low, q)
    total = jnp.sum(q[...] * ham[...], keepdims=True)
    rs = lax.rsqrt(jnp.maximum(total, 0.0) * (1.0 / 512) + 1e-6)
    expand(q, high, low)
    product(p, own, high, low, pq)
    z = w[own, :] - q[own, :] * rs + pq[...] * (0.25 * rs * rs)
    turn_blocks(rotation_weights(z.astype(BF16).astype(F32)), gt, gx, (o_ref, o_next, o_last))


def rotate(full, gt, gx):
    vmem = pl.BlockSpec(memory_space=pltpu.VMEM)
    return pl.pallas_call(
        rotate_kernel,
        out_shape=(jax.ShapeDtypeStruct((64, 2, 1024), BF16),) * 3,
        in_specs=[vmem] * 3,
        out_specs=(vmem,) * 3,
        scratch_shapes=[
            pltpu.VMEM((512, 1024), F32),
            pltpu.VMEM((512, 1024), F32),
            pltpu.VMEM((512, 1024), F32),
            pltpu.VMEM((512, 1024), F32),
            pltpu.VMEM((64, 1024), F32),
            pltpu.VMEM((1024, 1024), BF16),
            pltpu.VMEM((1024, 1024), BF16),
        ],
        compiler_params=pltpu.CompilerParams(vmem_limit_bytes=48 * 2**20),
    )(full, gt, gx)


def local(trial, applied, extra):
    rows, _, length = trial.shape
    scale = 1.0 / (length * lax.axis_size("ga"))
    gt, gx, z, ok = fast_filter(trial, applied, extra, scale)

    def planes(block):
        return jnp.swapaxes(block, 0, 1).reshape(2 * rows, length)

    def direct():
        margin = (trial.astype(F32) + extra.astype(F32)).astype(BF16)
        rest = jnp.concatenate([planes(applied), planes(margin)], axis=0)
        blocks, others, full = exchange(planes(trial), rest, scale)
        return tuple(rotate(full.reshape(2, 8, 512, 128), blocks, others))

    return lax.cond(ok[0, 0] > 0, lambda: tuple(fast_rotate(z, gt, gx)), direct)


def solution(mesh):
    spec = P("band", None, "ga")
    return jax.shard_map(local, mesh=mesh, in_specs=(spec,) * 3, out_specs=(spec,) * 3, check_vma=False)
```

```python
import functools

import jax
import jax.numpy as jnp
from jax import lax
from jax.experimental import pallas as pl
from jax.experimental.pallas import tpu as pltpu
from jax.sharding import PartitionSpec as P

MESH = pl.DeviceIdType.MESH
F32 = jnp.float32
BF16 = jnp.bfloat16


def iota(shape, dim):
    return lax.broadcasted_iota(jnp.int32, shape, dim)


def remote(src, dst, send_sem, recv_sem, device):
    return pltpu.make_async_remote_copy(
        src_ref=src,
        dst_ref=dst,
        send_sem=send_sem,
        recv_sem=recv_sem,
        device_id=device,
        device_id_type=MESH,
    )


def exchange_kernel(scale, t_ref, x_ref, gt_ref, gx_ref, full_ref, gt, part, core_in, mid, x_in, low, z_in, full,
                    t_send, t_recv, x_send, x_recv, s_send, s_recv, local_sem):
    g = lax.axis_index("ga")
    b = lax.axis_index("band")
    zl, x, c = g // 8, (g // 2) % 4, g % 2
    h, y = b // 4, b % 4
    partner = (1 - h) * 4 + y
    y_up, y_dn, y_far = (y + 1) % 4, (y + 3) % 4, (y + 2) % 4

    def band_at(hh, yy):
        return hh * 4 + yy

    def ga_at(zz, xx, cc):
        return zz * 8 + xx * 2 + cc

    barrier = pltpu.get_barrier_semaphore()
    greet = [(g, (b + d) % 8) for d in range(1, 8)]
    greet += [(ga_at(zl, x, 1 - c), b)]
    greet += [(ga_at(zl, (x + d) % 4, c), b) for d in range(1, 4)]
    greet += [(ga_at((zl + d) % 4, x, c), b) for d in range(1, 4)]
    for device in greet:
        pl.semaphore_signal(barrier, inc=1, device_id=device, device_id_type=MESH)
    pl.semaphore_wait(barrier, len(greet))

    up, dn, over = (g, band_at(h, y_up)), (g, band_at(h, y_dn)), (g, partner)

    def gather(own, slots, half, send, recv):
        def move(n, src, block, rows, device):
            return remote(src, slots.at[block, rows], send.at[n], recv.at[n], device)

        whole = pl.ds(0, 2 * half)
        lo, hi = pl.ds(0, half), pl.ds(half, half)
        b_dn, b_up = band_at(h, y_dn), band_at(h, y_up)
        p_dn, p_up = band_at(1 - h, y_dn), band_at(1 - h, y_up)
        first = [move(0, own, b, whole, over), move(1, own, b, whole, up), move(2, own, b, whole, dn)]
        second = [
            move(3, slots.at[partner], partner, whole, up),
            move(4, slots.at[partner], partner, whole, dn),
            move(5, slots.at[b_dn, lo], b_dn, lo, up),
            move(6, slots.at[b_up, hi], b_up, hi, dn),
            move(7, slots.at[p_dn, lo], p_dn, lo, up),
            move(8, slots.at[p_up, hi], p_up, hi, dn),
        ]

        def start():
            for copy in first:
                copy.start()

        def forward_own():
            first[1].wait_recv()
            second[2].start()
            first[2].wait_recv()
            second[3].start()

        def forward_partner():
            first[0].wait_recv()
            second[0].start()
            second[1].start()

        def forward_far():
            second[0].wait_recv()
            second[4].start()
            second[1].wait_recv()
            second[5].start()

        def finish():
            for copy in second[2:]:
                copy.wait_recv()

        def drain():
            for copy in first + second:
                copy.wait_send()

        return start, forward_own, forward_partner, forward_far, finish, drain

    t_start, t_own, t_partner, t_far, t_finish, t_drain = gather(t_ref, gt, 64, t_send, t_recv)
    x_start, x_own, x_partner, x_far, x_finish, x_drain = gather(x_ref, gx_ref, 128, x_send, x_recv)
    t_start()
    own_t = pltpu.make_async_copy(t_ref, gt.at[b], local_sem.at[0])
    own_t.start()
    own_x = pltpu.make_async_copy(x_ref, gx_ref.at[b], local_sem.at[1])
    own_x.start()
    own_t.wait()
    own_x.wait()
    t_own()
    t_partner()
    t_far()
    t_finish()
    t_drain()
    x_start()

    sign = jnp.where(iota((64, 128), 1) < 64, scale, -scale).astype(F32)

    def gram(k, carry):
        u = lax.dot_general(
            x_ref[...], gt[k], (((1,), (1,)), ((), ())), preferred_element_type=F32
        )
        part[1, k] = u[0:64] * sign + pltpu.roll(u[64:128], 64, 1) * scale
        part[0, k] = u[128:192] * sign + pltpu.roll(u[192:256], 64, 1) * scale
        return carry

    lax.fori_loop(0, 8, gram, 0)

    sib = (ga_at(zl, x, 1 - c), b)
    move = remote(part.at[:, pl.ds((1 - c) * 4, 4)], core_in, s_send.at[0], s_recv.at[0], sib)
    move.start()
    move.wait()
    mid[...] = part[:, pl.ds(c * 4, 4)] + core_in[...]

    moves = [
        remote(mid.at[:, (x + d) % 4], x_in.at[d - 1], s_send.at[d], s_recv.at[d], (ga_at(zl, (x + d) % 4, c), b))
        for d in range(1, 4)
    ]
    for move in moves:
        move.start()
    for move in moves:
        move.wait()
    low[...] = mid[:, x] + x_in[0] + x_in[1] + x_in[2]

    moves = [
        remote(
            low.at[:, pl.ds(((zl + d) % 4) * 16, 16)],
            z_in.at[d - 1],
            s_send.at[3 + d],
            s_recv.at[3 + d],
            (ga_at((zl + d) % 4, x, c), b),
        )
        for d in range(1, 4)
    ]
    for move in moves:
        move.start()
    for move in moves:
        move.wait()
    blk = c * 4 + x
    full[:, blk, b, zl] = low[:, pl.ds(zl * 16, 16)] + z_in[0] + z_in[1] + z_in[2]

    x_own()
    x_partner()

    def spread(view, base, devices):
        moves = [
            remote(view, view, s_send.at[base + n], s_recv.at[base + n], device) for n, device in enumerate(devices)
        ]
        for move in moves:
            move.start()
        for move in moves:
            move.wait()

    spread(full.at[:, blk, b, zl], 7, [(g, (b + d) % 8) for d in range(1, 8)])
    spread(full.at[:, blk, :, zl], 14, [(ga_at((zl + d) % 4, x, c), b) for d in range(1, 4)])
    spread(full.at[:, blk], 17, [(ga_at(zl, (x + d) % 4, c), b) for d in range(1, 4)])
    spread(full.at[:, pl.ds(c * 4, 4)], 20, [sib])

    out_t = pltpu.make_async_copy(gt, gt_ref, local_sem.at[0])
    out_f = pltpu.make_async_copy(full, full_ref, local_sem.at[1])
    out_t.start()
    out_f.start()
    x_far()
    x_finish()
    x_drain()
    out_t.wait()
    out_f.wait()


def exchange(trial, rest, scale):
    vmem = pl.BlockSpec(memory_space=pltpu.VMEM)
    anywhere = pl.BlockSpec(memory_space=pl.ANY)
    sem = pltpu.SemaphoreType.DMA
    return pl.pallas_call(
        functools.partial(exchange_kernel, scale),
        out_shape=(
            jax.ShapeDtypeStruct((8, 128, 1024), BF16),
            jax.ShapeDtypeStruct((8, 256, 1024), BF16),
            jax.ShapeDtypeStruct((2, 8, 8, 4, 16, 128), F32),
        ),
        in_specs=[vmem, vmem],
        out_specs=(anywhere, anywhere, anywhere),
        scratch_shapes=[
            pltpu.VMEM((8, 128, 1024), BF16),
            pltpu.VMEM((2, 8, 64, 128), F32),
            pltpu.VMEM((2, 4, 64, 128), F32),
            pltpu.VMEM((2, 4, 64, 128), F32),
            pltpu.VMEM((3, 2, 64, 128), F32),
            pltpu.VMEM((2, 64, 128), F32),
            pltpu.VMEM((3, 2, 16, 128), F32),
            pltpu.VMEM((2, 8, 8, 4, 16, 128), F32),
            sem((9,)),
            sem((9,)),
            sem((9,)),
            sem((9,)),
            sem((21,)),
            sem((21,)),
            sem((2,)),
        ],
        compiler_params=pltpu.CompilerParams(
            collective_id=0, has_side_effects=True, vmem_limit_bytes=48 * 2**20
        ),
    )(trial, rest)


def invert_pivot(block):
    lane, row = iota((64, 128), 1), iota((64, 128), 0)
    one = lane[:1]
    for k in range(0, 64, 2):
        m = k + 1
        c0r = jnp.broadcast_to(block[:, k : k + 1], (64, 128))
        c0i = jnp.broadcast_to(block[:, 64 + k : 65 + k], (64, 128))
        c1r = jnp.broadcast_to(block[:, m : m + 1], (64, 128))
        c1i = jnp.broadcast_to(block[:, 64 + m : 65 + m], (64, 128))
        r0, r1 = block[k : k + 1, :], block[m : m + 1, :]
        s0, s1 = pltpu.roll(r0, 64, 1), pltpu.roll(r1, 64, 1)
        s0, s1 = jnp.where(one < 64, -s0, s0), jnp.where(one < 64, -s1, s1)
        a, br, bi, c = c0r[k : k + 1], c1r[k : k + 1], c1i[k : k + 1], c1r[m : m + 1]
        e0, e0i, e1, e1i = one == k, one == 64 + k, one == m, one == 64 + m
        r0 = jnp.where(e0, 1.0, jnp.where(e0i | e1 | e1i, 0.0, r0))
        s0 = jnp.where(e0i, 1.0, jnp.where(e0 | e1 | e1i, 0.0, s0))
        r1 = jnp.where(e1, 1.0, jnp.where(e1i | e0 | e0i, 0.0, r1))
        s1 = jnp.where(e1i, 1.0, jnp.where(e1 | e0 | e0i, 0.0, s1))
        ra = 1.0 / a
        tr, ti = br * ra, bi * ra
        rs = 1.0 / (c - (br * br + bi * bi) * ra)
        i01r, i01i = -tr * rs, -ti * rs
        i00 = ra + (tr * tr + ti * ti) * rs
        q0 = i00 * r0 + i01r * r1 + i01i * s1
        q1 = i01r * r0 - i01i * s0 + rs * r1
        u0 = i00 * s0 + i01r * s1 - i01i * r1
        u1 = i01r * s0 + i01i * r0 + rs * s1
        isk, ism = row == k, row == m
        c0r = jnp.where(isk, -1.0, jnp.where(ism, 0.0, c0r))
        c1r = jnp.where(ism, -1.0, jnp.where(isk, 0.0, c1r))
        c0i, c1i = jnp.where(isk | ism, 0.0, c0i), jnp.where(isk | ism, 0.0, c1i)
        dead = isk | ism | (lane == k) | (lane == m) | (lane == 64 + k) | (lane == 64 + m)
        block = jnp.where(dead, 0.0, block) - c0r * q0 - c0i * u0 - c1r * q1 - c1i * u1
    return block


def halves(value):
    high = value.astype(BF16)
    return high, (value - high.astype(F32)).astype(BF16)


def dot(a, b):
    return jnp.dot(a, b, preferred_element_type=F32)


def dot_split(a, b):
    ah, al = halves(a)
    bh, bl = halves(b)
    return dot(ah, bh) + dot(al, bh) + dot(ah, bl)


def times_i(value):
    tiles = [pltpu.roll(value[:, n : n + 128], 64, 1) for n in range(0, value.shape[1], 128)]
    turned = jnp.concatenate(tiles, axis=1)
    return jnp.where(iota(value.shape, 1) % 128 < 64, -turned, turned)


def invert(work):
    def step(k, carry):
        rows, lanes = pl.ds(pl.multiple_of(k * 64, 64), 64), pl.ds(pl.multiple_of(k * 128, 128), 128)
        pivot = invert_pivot(work[rows, lanes])
        panel = work[rows, :]
        panel = dot_split(pivot, jnp.concatenate([panel, times_i(panel)], axis=0))
        panel = jnp.where(iota((64, 1024), 1) // 128 == k, jnp.concatenate([pivot] * 8, axis=1), panel)
        column = jnp.where(iota((512, 128), 0) // 64 == k, 0.0, work[:, lanes])
        work[:, lanes] = jnp.zeros((512, 128), F32)
        work[...] = work[...] - dot_split(column, jnp.concatenate([panel, times_i(panel)], axis=0))
        work[rows, :] = panel
        return carry

    lax.fori_loop(0, 8, step, 0)


def hermitian_part(full, m, out):
    lane = iota((64, 128), 1) < 64

    def row_block(k, carry):
        rows = pl.ds(pl.multiple_of(k * 64, 64), 64)
        for n in range(0, 8, 2):
            turned = full[m, k, pl.ds(64 * n, 128), :].T
            re, im = turned[0:64], -turned[64:128]
            left = jnp.where(lane, re, pltpu.roll(im, 64, 1))
            right = jnp.where(lane, pltpu.roll(re, 64, 1), im)
            out[rows, pl.ds(128 * n, 128)] = (full[m, n, rows, :] + left) * 0.5
            out[rows, pl.ds(128 * n + 128, 128)] = (full[m, n + 1, rows, :] + right) * 0.5
        return carry

    lax.fori_loop(0, 8, row_block, 0)


def expand(value_ref, high, low):
    def row_block(k, carry):
        rows = pl.ds(pl.multiple_of(k * 64, 64), 64)
        value = value_ref[rows, :]
        vh, vl = halves(value)
        th, tl = halves(times_i(value))
        top, bottom = pl.ds(pl.multiple_of(k * 128, 128), 64), pl.ds(pl.multiple_of(k * 128 + 64, 64), 64)
        high[top, :], high[bottom, :], low[top, :], low[bottom, :] = vh, th, vl, tl
        return carry

    lax.fori_loop(0, 8, row_block, 0)


def product(left_ref, rows, high, low, out):
    def column_block(n, carry):
        lanes = pl.ds(pl.multiple_of(n * 256, 256), 256)
        ah, al = halves(left_ref[rows, :])
        bh = high[:, lanes]
        out[:, lanes] = dot(ah, bh) + dot(al, bh) + dot(ah, low[:, lanes])
        return carry

    lax.fori_loop(0, 4, column_block, 0)


def unweave(to_planes):
    row, col = iota((128, 128), 0), iota((128, 128), 1)
    if not to_planes:
        row, col = col, row
    source = jnp.where(row < 64, 2 * row, 2 * row - 127)
    return jnp.where(col == source, 1.0, 0.0).astype(BF16)


def fast_kernel(scale, trial, applied, extra, gt_ref, gx_ref, z_ref, ok_ref, t_ref, x_ref, gt, part, core_in, mid, x_in,
                ring, full, dcol, drow, left_a, left_b, right_a, right_b, right_c, one, two, three, four, t_send,
                t_recv, x_send, x_recv, s_send, s_recv, local_sem):
    g = lax.axis_index("ga")
    b = lax.axis_index("band")
    zl, x, c = g // 8, (g // 2) % 4, g % 2
    h, y = b // 4, b % 4
    partner = (1 - h) * 4 + y
    y_up, y_dn, y_far = (y + 1) % 4, (y + 3) % 4, (y + 2) % 4

    def band_at(hh, yy):
        return hh * 4 + yy

    def ga_at(zz, xx, cc):
        return zz * 8 + xx * 2 + cc

    def ring_at(d):
        z = (h * 4 + zl + d) % 8
        return (ga_at(z % 4, x, c), band_at(z // 4, y))

    sib = (ga_at(zl, x, 1 - c), b)
    xs = [(ga_at(zl, (x + d) % 4, c), b) for d in range(1, 4)]
    ys = [(g, band_at(h, (y + d) % 4)) for d in range(1, 4)]
    rings = [ring_at(d) for d in range(1, 8)]
    barrier = pltpu.get_barrier_semaphore()
    greet = [sib] + xs + ys + rings
    for device in greet:
        pl.semaphore_signal(barrier, inc=1, device_id=device, device_id_type=MESH)
    planes = unweave(True)
    t_ref[...] = dot(planes, trial[...].reshape(128, 1024)).astype(BF16)
    pl.semaphore_wait(barrier, len(greet))

    up, dn, over = (g, band_at(h, y_up)), (g, band_at(h, y_dn)), (g, partner)
    b_dn, b_up, b_far = band_at(h, y_dn), band_at(h, y_up), band_at(h, y_far)
    p_dn, p_up, p_far = band_at(1 - h, y_dn), band_at(1 - h, y_up), band_at(1 - h, y_far)

    class Gather:
        def __init__(self, own, slots, size, send, recv):
            def move(n, src, block, rows, device):
                return remote(src, slots.at[block, rows], send.at[n], recv.at[n], device)

            def relay(n, block, rows, device):
                return move(n, slots.at[block, rows], block, rows, device)

            step = size // 4
            piece = [pl.ds(n * step, step) for n in range(4)]
            whole, lo, hi = pl.ds(0, size), pl.ds(0, size // 2), pl.ds(size // 2, size // 2)
            self.cross = [move(n, own.at[piece[n]], b, piece[n], over) for n in range(4)]
            self.near = [move(4, own, b, whole, up), move(5, own, b, whole, dn)]
            self.far = [relay(6, b_dn, lo, up), relay(7, b_up, hi, dn)]
            self.to_up = [relay(8 + n, partner, piece[n], up) for n in range(4)]
            self.to_dn = [relay(12 + n, partner, piece[n], dn) for n in range(4)]
            self.last = [relay(16, p_dn, piece[0], up), relay(17, p_dn, piece[1], up)]
            self.last += [relay(18, p_up, piece[2], dn), relay(19, p_up, piece[3], dn)]

        def start_near(self):
            for copy in self.near:
                copy.start()

        def start_cross(self, first, count):
            for copy in self.cross[first : first + count]:
                copy.start()

        def pass_own(self):
            for n in range(2):
                self.near[n].wait_recv()
                self.far[n].start()

        def pass_cross(self, n):
            self.cross[n].wait_recv()
            self.to_up[n].start()
            self.to_dn[n].start()

        def pass_last(self, n):
            (self.to_up if n < 2 else self.to_dn)[n].wait_recv()
            self.last[n].start()

        def finish(self):
            for copy in self.far + self.to_up[2:] + self.to_dn[:2] + self.last:
                copy.wait_recv()

        def drain(self):
            for copy in self.cross + self.near + self.far + self.to_up + self.to_dn + self.last:
                copy.wait_send()

    tg = Gather(t_ref, gt, 128, t_send, t_recv)
    xg = Gather(x_ref, gx_ref, 256, x_send, x_recv)

    sign = jnp.where(iota((64, 128), 1) < 64, scale, -scale).astype(F32)

    def gram(k, block):
        u = lax.dot_general(x_ref[...], block, (((1,), (1,)), ((), ())), preferred_element_type=F32)
        part[1, k] = u[0:64] * sign + pltpu.roll(u[64:128], 64, 1) * scale
        part[0, k] = u[128:192] * sign + pltpu.roll(u[192:256], 64, 1) * scale

    tg.start_cross(0, 1)
    tg.start_near()
    tg.start_cross(1, 3)
    x_ref[0:128] = dot(planes, applied[...].reshape(128, 1024)).astype(BF16)
    margin = (trial[...].astype(F32) + extra[...].astype(F32)).astype(BF16)
    x_ref[128:256] = dot(planes, margin.reshape(128, 1024)).astype(BF16)
    own_x = pltpu.make_async_copy(x_ref, gx_ref.at[b], local_sem.at[1])
    own_x.start()
    gt[b] = t_ref[...]
    gram(b, t_ref[...])
    tg.pass_cross(0)
    tg.pass_own()
    tg.pass_cross(1)
    tg.pass_last(0)
    tg.pass_cross(2)
    tg.pass_last(1)
    tg.pass_cross(3)
    xg.start_cross(0, 2)
    gram(b_dn, gt[b_dn])
    gram(b_up, gt[b_up])
    gram(partner, gt[partner])
    tg.pass_last(2)
    tg.pass_last(3)
    xg.start_near()
    tg.finish()
    for k in (b_far, p_dn, p_up, p_far):
        gram(k, gt[k])

    blk = c * 4 + x
    lane64 = iota((64, 128), 1) < 64
    eye = iota((64, 128), 0) == iota((64, 128), 1)
    eye_im = iota((64, 128), 0) + 64 == iota((64, 128), 1)

    def rounded(value):
        return value.astype(BF16).astype(F32)

    def core_moves(m):
        return [remote(part.at[m, pl.ds((1 - c) * 4, 4)], core_in.at[m], s_send.at[m, 0], s_recv.at[m, 0], sib)]

    def core_add(m):
        mid[m] = part[m, pl.ds(c * 4, 4)] + core_in[m]

    def x_moves(m):
        return [
            remote(mid.at[m, (x + d) % 4], x_in.at[m, d - 1], s_send.at[m, d], s_recv.at[m, d], xs[d - 1])
            for d in range(1, 4)
        ]

    def x_add(m):
        value = mid[m, x] + x_in[m, 0] + x_in[m, 1] + x_in[m, 2]
        turned = pltpu.roll(value, 64, 1)
        ring[m, h, zl] = jnp.where(eye_im & (blk == b), turned - rounded(turned), value).astype(BF16)

    def spread(m, view, base, devices):
        return [
            remote(view, view, s_send.at[m, base + n], s_recv.at[m, base + n], device)
            for n, device in enumerate(devices)
        ]

    def ring_add(m):
        for hh in range(2):
            value = ring[m, hh, 0].astype(F32)
            for n in range(1, 4):
                value = value + ring[m, hh, n].astype(F32)
            exact = value + pltpu.roll(value, 64, 1)
            mine = blk == hh * 4 + y
            value = jnp.where(eye & mine, exact, jnp.where(eye_im & mine, exact - rounded(exact), value))
            full[m, blk, hh, y] = value.astype(BF16)

    stages = [
        (core_moves, core_add),
        (x_moves, x_add),
        (lambda m: spread(m, ring.at[m, h, zl], 4, rings), ring_add),
        (lambda m: spread(m, full.at[m, blk, :, y], 11, ys), None),
        (lambda m: spread(m, full.at[m, blk], 14, xs), None),
        (lambda m: spread(m, full.at[m, pl.ds(c * 4, 4)], 17, [sib]), None),
    ]
    flight = {}

    def launch(n, m):
        flight[n, m] = stages[n][0](m)
        for move in flight[n, m]:
            move.start()

    def land(n, m):
        for move in flight[n, m]:
            move.wait()
        if stages[n][1] is not None:
            stages[n][1](m)

    def turn(n):
        land(n, 0)
        launch(n + 1, 0)
        land(n, 1)
        launch(n + 1, 1)

    launch(0, 0)
    out_t = pltpu.make_async_copy(gt, gt_ref, local_sem.at[0])
    out_t.start()
    land(0, 0)
    launch(1, 0)
    launch(0, 1)
    land(1, 0)
    launch(2, 0)
    land(0, 1)
    launch(1, 1)
    land(2, 0)
    launch(3, 0)
    land(1, 1)
    launch(2, 1)
    land(3, 0)
    launch(4, 0)
    land(2, 1)
    launch(3, 1)
    xg.start_cross(2, 2)
    xg.pass_own()
    xg.pass_cross(0)
    xg.pass_cross(1)
    land(4, 0)
    launch(5, 0)
    land(3, 1)
    launch(4, 1)
    land(5, 0)

    def tile(m, n, k, count):
        block = full[m, n, k // 4, pl.ds(k % 4, count)]
        return block.astype(F32).reshape(64 * count, 128)

    def scales(k, carry):
        rows = pl.ds(pl.multiple_of(k * 64, 64), 64)
        block = tile(0, k, k, 1)
        diagonal = jnp.where(eye, block + pltpu.roll(block, 64, 1), 0.0)
        dcol[rows, :] = jnp.broadcast_to(lax.rsqrt(jnp.sum(diagonal, axis=1, keepdims=True)), (64, 128))
        across = jnp.sum(diagonal, axis=0, keepdims=True)
        across = lax.rsqrt(across + pltpu.roll(across, 64, 1))
        drow[:, pl.ds(pl.multiple_of(k * 128, 128), 128)] = jnp.broadcast_to(across, (8, 128))
        return carry

    lax.fori_loop(0, 8, scales, 0, unroll=True)

    def scaled_rows(m, k, factor, out, left_out, right_out):
        rows = pl.ds(pl.multiple_of(k * 64, 64), 64)
        top, bottom = pl.ds(pl.multiple_of(k * 128, 128), 64), pl.ds(pl.multiple_of(k * 128 + 64, 64), 64)
        left = dcol[rows, :] * (0.5 * factor)
        for n in range(0, 8, 2):
            turned = tile(m, k, n, 2).T
            re, im = turned[0:64], -turned[64:128]
            back = (
                jnp.where(lane64, re, pltpu.roll(im, 64, 1)),
                jnp.where(lane64, pltpu.roll(re, 64, 1), im),
            )
            for i in range(2):
                lanes = pl.ds(128 * (n + i), 128)
                right = drow[0:1, lanes]
                block = tile(m, n + i, k, 1)
                value = (block + back[i]) * left * right
                if m == 0:
                    value = jnp.where((eye | eye_im) & (k == n + i), 0.0, value)
                    left_out[rows, lanes] = value.astype(BF16)
                else:
                    exact = (block + pltpu.roll(block, 64, 1)) * 2.0 * left * right
                    value = jnp.where(eye & (k == n + i), exact, value)
                    value = jnp.where(eye_im & (k == n + i), 0.0, value)
                out[rows, lanes] = value
                right_out[top, lanes] = value.astype(BF16)
                right_out[bottom, lanes] = times_i(value).astype(BF16)

    def put_right(right, lanes, value):
        turned = times_i(value)
        for k in range(8):
            rows = slice(64 * k, 64 * k + 64)
            right[pl.ds(128 * k, 64), lanes] = value[rows].astype(BF16)
            right[pl.ds(128 * k + 64, 64), lanes] = turned[rows].astype(BF16)

    def by_columns(body, init=0):
        def column_block(n, carry):
            return body(n, pl.ds(pl.multiple_of(n * 256, 256), 256), carry)

        return lax.fori_loop(0, 4, column_block, init, unroll=True)

    def column_sum(value):
        return jnp.sum(value, axis=0, keepdims=True)

    zero_row = jnp.zeros((1, 256), F32)

    def margin_rows(k, carry):
        scaled_rows(0, k, -1.0, one, left_a, right_a)
        return carry

    lax.fori_loop(0, 8, margin_rows, 0)
    xg.pass_cross(2)
    land(4, 1)
    launch(5, 1)

    def second_power(n, lanes, carry):
        value = dot(left_a[...], right_a[:, lanes])
        two[:, lanes] = value
        put_right(right_b, lanes, value + one[:, lanes])
        return carry

    by_columns(second_power)
    xg.pass_cross(3)
    xg.pass_last(0)
    land(5, 1)

    def third_power(n, lanes, carry):
        value = dot(left_a[...], right_b[:, lanes])
        cube = value - two[:, lanes]
        left_b[:, lanes] = cube.astype(BF16)
        one[:, lanes] = one[:, lanes] + value
        scaled_rows(1, 2 * n, 1.0, four, None, right_c)
        scaled_rows(1, 2 * n + 1, 1.0, four, None, right_c)
        return carry + column_sum(cube * cube)

    cube_norm = by_columns(third_power, zero_row)
    xg.pass_last(1)

    def series(n, lanes, carry):
        value = one[:, lanes] + dot(left_b[...], right_b[:, lanes])
        two[:, lanes] = value
        left_a[:, lanes] = value.astype(BF16)
        put_right(right_a, lanes, value)
        return carry

    by_columns(series)
    xg.pass_last(2)
    xg.pass_last(3)

    def first_product(n, lanes, carry):
        value = four[:, lanes] + dot(left_a[...], right_c[:, lanes])
        one[:, lanes] = value
        left_b[:, lanes] = value.astype(BF16)
        return carry

    by_columns(first_product)

    def second_product(n, lanes, carry):
        value = one[:, lanes] + dot(left_b[...], right_a[:, lanes])
        three[:, lanes] = value
        put_right(right_b, lanes, value)
        return (carry[0] + column_sum(value * four[:, lanes]), carry[1] + column_sum(value * one[:, lanes]))

    sums = by_columns(second_product, (zero_row, zero_row))
    trace_qh = jnp.sum(sums[0], keepdims=True)
    trace_pq = jnp.sum(sums[1], keepdims=True)
    rs = lax.rsqrt(jnp.maximum(trace_qh, 0.0) * (1.0 / 512) + 1e-6)
    own = pl.ds(pl.multiple_of(b * 64, 64), 64)
    own_lanes = pl.ds(pl.multiple_of(b * 128, 128), 128)
    product = dot(left_b[own, :], right_b[...])
    four[own, :] = two[own, :] - three[own, :] * rs + product * (0.25 * rs * rs)
    four[own, own_lanes] = four[own, own_lanes] + jnp.where(eye, 1.0, 0.0)
    left = jnp.concatenate([dcol[own, :]] * 8, axis=1)
    z_ref[...] = rotation_weights(rounded(four[own, :] * left * drow[0:1, :]))

    def trace_of(ref):
        total = jnp.zeros((64, 128), F32)
        for k in range(8):
            total = total + jnp.where(eye, ref[pl.ds(k * 64, 64), pl.ds(k * 128, 128)], 0.0)
        return jnp.sum(total, keepdims=True)

    trace_w = 512.0 + trace_of(two)
    trace_z = trace_w - trace_of(three) * rs + trace_pq * (0.25 * rs * rs)
    small = jnp.sum(cube_norm, keepdims=True) < 0.0225
    ok = small & (trace_z > 0.6 * trace_w)
    ok_ref[...] = jnp.broadcast_to(jnp.where(ok, 1, 0).astype(jnp.int32), (8, 128))

    xg.finish()
    tg.drain()
    xg.drain()
    own_x.wait()
    out_t.wait()


def fast_filter(trial, applied, extra, scale):
    vmem = pl.BlockSpec(memory_space=pltpu.VMEM)
    anywhere = pl.BlockSpec(memory_space=pl.ANY)
    sem = pltpu.SemaphoreType.DMA
    square = pltpu.VMEM((512, 1024), F32)
    left = pltpu.VMEM((512, 1024), BF16)
    right = pltpu.VMEM((1024, 1024), BF16)
    return pl.pallas_call(
        functools.partial(fast_kernel, scale),
        out_shape=(
            jax.ShapeDtypeStruct((8, 128, 1024), BF16),
            jax.ShapeDtypeStruct((8, 256, 1024), BF16),
            jax.ShapeDtypeStruct((128, 1024), BF16),
            jax.ShapeDtypeStruct((8, 128), jnp.int32),
        ),
        in_specs=[vmem] * 3,
        out_specs=(anywhere, anywhere, vmem, vmem),
        scratch_shapes=[
            pltpu.VMEM((128, 1024), BF16),
            pltpu.VMEM((256, 1024), BF16),
            pltpu.VMEM((8, 128, 1024), BF16),
            pltpu.VMEM((2, 8, 64, 128), F32),
            pltpu.VMEM((2, 4, 64, 128), F32),
            pltpu.VMEM((2, 4, 64, 128), F32),
            pltpu.VMEM((2, 3, 64, 128), F32),
            pltpu.VMEM((2, 2, 4, 64, 128), BF16),
            pltpu.VMEM((2, 8, 2, 4, 64, 128), BF16),
            pltpu.VMEM((512, 128), F32),
            pltpu.VMEM((8, 1024), F32),
            left,
            left,
            right,
            right,
            right,
            square,
            square,
            square,
            square,
            sem((20,)),
            sem((20,)),
            sem((20,)),
            sem((20,)),
            sem((2, 18)),
            sem((2, 18)),
            sem((2,)),
        ],
        compiler_params=pltpu.CompilerParams(
            collective_id=1, has_side_effects=True, vmem_limit_bytes=48 * 2**20
        ),
    )(trial, applied, extra)


def rotation_weights(z):
    turned = times_i(z)
    re_part = jnp.where(iota((64, 1024), 1) % 128 < 64, z, -z)
    im_part = jnp.where(iota((64, 1024), 1) % 128 < 64, -turned, turned)
    both = jnp.concatenate([re_part, im_part], axis=0).astype(BF16)
    return dot(unweave(False), both).astype(BF16)


def turn_blocks(weights, gt, gx, outs):
    width = gt.shape[2]
    sources = (gt[...], gx[:, 0:128, :], gx[:, 128:256, :])
    for out, source in zip(outs, sources):
        value = dot(weights, source.reshape(1024, width)).astype(BF16)
        out[...] = value.reshape(64, 2, width)


def fast_rotate_kernel(z_ref, gt, gx, *outs):
    turn_blocks(z_ref[...], gt, gx, outs)


def fast_rotate(z, gt, gx):
    width = 512
    return pl.pallas_call(
        fast_rotate_kernel,
        grid=(1024 // width,),
        out_shape=(jax.ShapeDtypeStruct((64, 2, 1024), BF16),) * 3,
        in_specs=[
            pl.BlockSpec((128, 1024), lambda n: (0, 0)),
            pl.BlockSpec((8, 128, width), lambda n: (0, 0, n)),
            pl.BlockSpec((8, 256, width), lambda n: (0, 0, n)),
        ],
        out_specs=(pl.BlockSpec((64, 2, width), lambda n: (0, 0, n)),) * 3,
        compiler_params=pltpu.CompilerParams(vmem_limit_bytes=48 * 2**20),
    )(z, gt, gx)


def rotate_kernel(full, gt, gx, o_ref, o_next, o_last, w, ham, p, q, pq, high, low):
    b = lax.axis_index("band")
    own = pl.ds(pl.multiple_of(b * 64, 64), 64)
    hermitian_part(full, 0, w)
    hermitian_part(full, 1, ham)
    invert(w)
    expand(ham, high, low)
    product(w, pl.ds(0, 512), high, low, p)
    expand(w, high, low)
    product(p, pl.ds(0, 512), high, low, q)
    total = jnp.sum(q[...] * ham[...], keepdims=True)
    rs = lax.rsqrt(jnp.maximum(total, 0.0) * (1.0 / 512) + 1e-6)
    expand(q, high, low)
    product(p, own, high, low, pq)
    z = w[own, :] - q[own, :] * rs + pq[...] * (0.25 * rs * rs)
    turn_blocks(rotation_weights(z.astype(BF16).astype(F32)), gt, gx, (o_ref, o_next, o_last))


def rotate(full, gt, gx):
    vmem = pl.BlockSpec(memory_space=pltpu.VMEM)
    return pl.pallas_call(
        rotate_kernel,
        out_shape=(jax.ShapeDtypeStruct((64, 2, 1024), BF16),) * 3,
        in_specs=[vmem] * 3,
        out_specs=(vmem,) * 3,
        scratch_shapes=[
            pltpu.VMEM((512, 1024), F32),
            pltpu.VMEM((512, 1024), F32),
            pltpu.VMEM((512, 1024), F32),
            pltpu.VMEM((512, 1024), F32),
            pltpu.VMEM((64, 1024), F32),
            pltpu.VMEM((1024, 1024), BF16),
            pltpu.VMEM((1024, 1024), BF16),
        ],
        compiler_params=pltpu.CompilerParams(vmem_limit_bytes=48 * 2**20),
    )(full, gt, gx)


def local(trial, applied, extra):
    rows, _, length = trial.shape
    scale = 1.0 / (length * lax.axis_size("ga"))
    gt, gx, z, ok = fast_filter(trial, applied, extra, scale)

    def planes(block):
        return jnp.swapaxes(block, 0, 1).reshape(2 * rows, length)

    def direct():
        margin = (trial.astype(F32) + extra.astype(F32)).astype(BF16)
        rest = jnp.concatenate([planes(applied), planes(margin)], axis=0)
        blocks, others, full = exchange(planes(trial), rest, scale)
        return tuple(rotate(full.reshape(2, 8, 512, 128), blocks, others))

    return lax.cond(ok[0, 0] > 0, lambda: tuple(fast_rotate(z, gt, gx)), direct)


def solution(mesh):
    spec = P("band", None, "ga")
    return jax.shard_map(local, mesh=mesh, in_specs=(spec,) * 3, out_specs=(spec,) * 3, check_vma=False)
```

```python
import functools

import jax
import jax.numpy as jnp
from jax import lax
from jax.experimental import pallas as pl
from jax.experimental.pallas import tpu as pltpu
from jax.sharding import PartitionSpec as P

MESH = pl.DeviceIdType.MESH
F32 = jnp.float32
BF16 = jnp.bfloat16


def iota(shape, dim):
    return lax.broadcasted_iota(jnp.int32, shape, dim)


def remote(src, dst, send_sem, recv_sem, device):
    return pltpu.make_async_remote_copy(
        src_ref=src,
        dst_ref=dst,
        send_sem=send_sem,
        recv_sem=recv_sem,
        device_id=device,
        device_id_type=MESH,
    )


def exchange_kernel(scale, t_ref, x_ref, gt_ref, gx_ref, full_ref, gt, part, core_in, mid, x_in, low, z_in, full,
                    t_send, t_recv, x_send, x_recv, s_send, s_recv, local_sem):
    g = lax.axis_index("ga")
    b = lax.axis_index("band")
    zl, x, c = g // 8, (g // 2) % 4, g % 2
    h, y = b // 4, b % 4
    partner = (1 - h) * 4 + y
    y_up, y_dn, y_far = (y + 1) % 4, (y + 3) % 4, (y + 2) % 4

    def band_at(hh, yy):
        return hh * 4 + yy

    def ga_at(zz, xx, cc):
        return zz * 8 + xx * 2 + cc

    barrier = pltpu.get_barrier_semaphore()
    greet = [(g, (b + d) % 8) for d in range(1, 8)]
    greet += [(ga_at(zl, x, 1 - c), b)]
    greet += [(ga_at(zl, (x + d) % 4, c), b) for d in range(1, 4)]
    greet += [(ga_at((zl + d) % 4, x, c), b) for d in range(1, 4)]
    for device in greet:
        pl.semaphore_signal(barrier, inc=1, device_id=device, device_id_type=MESH)
    pl.semaphore_wait(barrier, len(greet))

    up, dn, over = (g, band_at(h, y_up)), (g, band_at(h, y_dn)), (g, partner)

    def gather(own, slots, half, send, recv):
        def move(n, src, block, rows, device):
            return remote(src, slots.at[block, rows], send.at[n], recv.at[n], device)

        whole = pl.ds(0, 2 * half)
        lo, hi = pl.ds(0, half), pl.ds(half, half)
        b_dn, b_up = band_at(h, y_dn), band_at(h, y_up)
        p_dn, p_up = band_at(1 - h, y_dn), band_at(1 - h, y_up)
        first = [move(0, own, b, whole, over), move(1, own, b, whole, up), move(2, own, b, whole, dn)]
        second = [
            move(3, slots.at[partner], partner, whole, up),
            move(4, slots.at[partner], partner, whole, dn),
            move(5, slots.at[b_dn, lo], b_dn, lo, up),
            move(6, slots.at[b_up, hi], b_up, hi, dn),
            move(7, slots.at[p_dn, lo], p_dn, lo, up),
            move(8, slots.at[p_up, hi], p_up, hi, dn),
        ]

        def start():
            for copy in first:
                copy.start()

        def forward_own():
            first[1].wait_recv()
            second[2].start()
            first[2].wait_recv()
            second[3].start()

        def forward_partner():
            first[0].wait_recv()
            second[0].start()
            second[1].start()

        def forward_far():
            second[0].wait_recv()
            second[4].start()
            second[1].wait_recv()
            second[5].start()

        def finish():
            for copy in second[2:]:
                copy.wait_recv()

        def drain():
            for copy in first + second:
                copy.wait_send()

        return start, forward_own, forward_partner, forward_far, finish, drain

    t_start, t_own, t_partner, t_far, t_finish, t_drain = gather(t_ref, gt, 64, t_send, t_recv)
    x_start, x_own, x_partner, x_far, x_finish, x_drain = gather(x_ref, gx_ref, 128, x_send, x_recv)
    t_start()
    own_t = pltpu.make_async_copy(t_ref, gt.at[b], local_sem.at[0])
    own_t.start()
    own_x = pltpu.make_async_copy(x_ref, gx_ref.at[b], local_sem.at[1])
    own_x.start()
    own_t.wait()
    own_x.wait()
    t_own()
    t_partner()
    t_far()
    t_finish()
    t_drain()
    x_start()

    sign = jnp.where(iota((64, 128), 1) < 64, scale, -scale).astype(F32)

    def gram(k, carry):
        u = lax.dot_general(
            x_ref[...], gt[k], (((1,), (1,)), ((), ())), preferred_element_type=F32
        )
        part[1, k] = u[0:64] * sign + pltpu.roll(u[64:128], 64, 1) * scale
        part[0, k] = u[128:192] * sign + pltpu.roll(u[192:256], 64, 1) * scale
        return carry

    lax.fori_loop(0, 8, gram, 0)

    sib = (ga_at(zl, x, 1 - c), b)
    move = remote(part.at[:, pl.ds((1 - c) * 4, 4)], core_in, s_send.at[0], s_recv.at[0], sib)
    move.start()
    move.wait()
    mid[...] = part[:, pl.ds(c * 4, 4)] + core_in[...]

    moves = [
        remote(mid.at[:, (x + d) % 4], x_in.at[d - 1], s_send.at[d], s_recv.at[d], (ga_at(zl, (x + d) % 4, c), b))
        for d in range(1, 4)
    ]
    for move in moves:
        move.start()
    for move in moves:
        move.wait()
    low[...] = mid[:, x] + x_in[0] + x_in[1] + x_in[2]

    moves = [
        remote(
            low.at[:, pl.ds(((zl + d) % 4) * 16, 16)],
            z_in.at[d - 1],
            s_send.at[3 + d],
            s_recv.at[3 + d],
            (ga_at((zl + d) % 4, x, c), b),
        )
        for d in range(1, 4)
    ]
    for move in moves:
        move.start()
    for move in moves:
        move.wait()
    blk = c * 4 + x
    full[:, blk, b, zl] = low[:, pl.ds(zl * 16, 16)] + z_in[0] + z_in[1] + z_in[2]

    x_own()
    x_partner()

    def spread(view, base, devices):
        moves = [
            remote(view, view, s_send.at[base + n], s_recv.at[base + n], device) for n, device in enumerate(devices)
        ]
        for move in moves:
            move.start()
        for move in moves:
            move.wait()

    spread(full.at[:, blk, b, zl], 7, [(g, (b + d) % 8) for d in range(1, 8)])
    spread(full.at[:, blk, :, zl], 14, [(ga_at((zl + d) % 4, x, c), b) for d in range(1, 4)])
    spread(full.at[:, blk], 17, [(ga_at(zl, (x + d) % 4, c), b) for d in range(1, 4)])
    spread(full.at[:, pl.ds(c * 4, 4)], 20, [sib])

    out_t = pltpu.make_async_copy(gt, gt_ref, local_sem.at[0])
    out_f = pltpu.make_async_copy(full, full_ref, local_sem.at[1])
    out_t.start()
    out_f.start()
    x_far()
    x_finish()
    x_drain()
    out_t.wait()
    out_f.wait()


def exchange(trial, rest, scale):
    vmem = pl.BlockSpec(memory_space=pltpu.VMEM)
    anywhere = pl.BlockSpec(memory_space=pl.ANY)
    sem = pltpu.SemaphoreType.DMA
    return pl.pallas_call(
        functools.partial(exchange_kernel, scale),
        out_shape=(
            jax.ShapeDtypeStruct((8, 128, 1024), BF16),
            jax.ShapeDtypeStruct((8, 256, 1024), BF16),
            jax.ShapeDtypeStruct((2, 8, 8, 4, 16, 128), F32),
        ),
        in_specs=[vmem, vmem],
        out_specs=(anywhere, anywhere, anywhere),
        scratch_shapes=[
            pltpu.VMEM((8, 128, 1024), BF16),
            pltpu.VMEM((2, 8, 64, 128), F32),
            pltpu.VMEM((2, 4, 64, 128), F32),
            pltpu.VMEM((2, 4, 64, 128), F32),
            pltpu.VMEM((3, 2, 64, 128), F32),
            pltpu.VMEM((2, 64, 128), F32),
            pltpu.VMEM((3, 2, 16, 128), F32),
            pltpu.VMEM((2, 8, 8, 4, 16, 128), F32),
            sem((9,)),
            sem((9,)),
            sem((9,)),
            sem((9,)),
            sem((21,)),
            sem((21,)),
            sem((2,)),
        ],
        compiler_params=pltpu.CompilerParams(
            collective_id=0, has_side_effects=True, vmem_limit_bytes=48 * 2**20
        ),
    )(trial, rest)


def invert_pivot(block):
    lane, row = iota((64, 128), 1), iota((64, 128), 0)
    one = lane[:1]
    for k in range(0, 64, 2):
        m = k + 1
        c0r = jnp.broadcast_to(block[:, k : k + 1], (64, 128))
        c0i = jnp.broadcast_to(block[:, 64 + k : 65 + k], (64, 128))
        c1r = jnp.broadcast_to(block[:, m : m + 1], (64, 128))
        c1i = jnp.broadcast_to(block[:, 64 + m : 65 + m], (64, 128))
        r0, r1 = block[k : k + 1, :], block[m : m + 1, :]
        s0, s1 = pltpu.roll(r0, 64, 1), pltpu.roll(r1, 64, 1)
        s0, s1 = jnp.where(one < 64, -s0, s0), jnp.where(one < 64, -s1, s1)
        a, br, bi, c = c0r[k : k + 1], c1r[k : k + 1], c1i[k : k + 1], c1r[m : m + 1]
        e0, e0i, e1, e1i = one == k, one == 64 + k, one == m, one == 64 + m
        r0 = jnp.where(e0, 1.0, jnp.where(e0i | e1 | e1i, 0.0, r0))
        s0 = jnp.where(e0i, 1.0, jnp.where(e0 | e1 | e1i, 0.0, s0))
        r1 = jnp.where(e1, 1.0, jnp.where(e1i | e0 | e0i, 0.0, r1))
        s1 = jnp.where(e1i, 1.0, jnp.where(e1 | e0 | e0i, 0.0, s1))
        ra = 1.0 / a
        tr, ti = br * ra, bi * ra
        rs = 1.0 / (c - (br * br + bi * bi) * ra)
        i01r, i01i = -tr * rs, -ti * rs
        i00 = ra + (tr * tr + ti * ti) * rs
        q0 = i00 * r0 + i01r * r1 + i01i * s1
        q1 = i01r * r0 - i01i * s0 + rs * r1
        u0 = i00 * s0 + i01r * s1 - i01i * r1
        u1 = i01r * s0 + i01i * r0 + rs * s1
        isk, ism = row == k, row == m
        c0r = jnp.where(isk, -1.0, jnp.where(ism, 0.0, c0r))
        c1r = jnp.where(ism, -1.0, jnp.where(isk, 0.0, c1r))
        c0i, c1i = jnp.where(isk | ism, 0.0, c0i), jnp.where(isk | ism, 0.0, c1i)
        dead = isk | ism | (lane == k) | (lane == m) | (lane == 64 + k) | (lane == 64 + m)
        block = jnp.where(dead, 0.0, block) - c0r * q0 - c0i * u0 - c1r * q1 - c1i * u1
    return block


def halves(value):
    high = value.astype(BF16)
    return high, (value - high.astype(F32)).astype(BF16)


def dot(a, b):
    return jnp.dot(a, b, preferred_element_type=F32)


def dot_split(a, b):
    ah, al = halves(a)
    bh, bl = halves(b)
    return dot(ah, bh) + dot(al, bh) + dot(ah, bl)


def times_i(value):
    tiles = [pltpu.roll(value[:, n : n + 128], 64, 1) for n in range(0, value.shape[1], 128)]
    turned = jnp.concatenate(tiles, axis=1)
    return jnp.where(iota(value.shape, 1) % 128 < 64, -turned, turned)


def invert(work):
    def step(k, carry):
        rows, lanes = pl.ds(pl.multiple_of(k * 64, 64), 64), pl.ds(pl.multiple_of(k * 128, 128), 128)
        pivot = invert_pivot(work[rows, lanes])
        panel = work[rows, :]
        panel = dot_split(pivot, jnp.concatenate([panel, times_i(panel)], axis=0))
        panel = jnp.where(iota((64, 1024), 1) // 128 == k, jnp.concatenate([pivot] * 8, axis=1), panel)
        column = jnp.where(iota((512, 128), 0) // 64 == k, 0.0, work[:, lanes])
        work[:, lanes] = jnp.zeros((512, 128), F32)
        work[...] = work[...] - dot_split(column, jnp.concatenate([panel, times_i(panel)], axis=0))
        work[rows, :] = panel
        return carry

    lax.fori_loop(0, 8, step, 0)


def hermitian_part(full, m, out):
    lane = iota((64, 128), 1) < 64

    def row_block(k, carry):
        rows = pl.ds(pl.multiple_of(k * 64, 64), 64)
        for n in range(0, 8, 2):
            turned = full[m, k, pl.ds(64 * n, 128), :].T
            re, im = turned[0:64], -turned[64:128]
            left = jnp.where(lane, re, pltpu.roll(im, 64, 1))
            right = jnp.where(lane, pltpu.roll(re, 64, 1), im)
            out[rows, pl.ds(128 * n, 128)] = (full[m, n, rows, :] + left) * 0.5
            out[rows, pl.ds(128 * n + 128, 128)] = (full[m, n + 1, rows, :] + right) * 0.5
        return carry

    lax.fori_loop(0, 8, row_block, 0)


def expand(value_ref, high, low):
    def row_block(k, carry):
        rows = pl.ds(pl.multiple_of(k * 64, 64), 64)
        value = value_ref[rows, :]
        vh, vl = halves(value)
        th, tl = halves(times_i(value))
        top, bottom = pl.ds(pl.multiple_of(k * 128, 128), 64), pl.ds(pl.multiple_of(k * 128 + 64, 64), 64)
        high[top, :], high[bottom, :], low[top, :], low[bottom, :] = vh, th, vl, tl
        return carry

    lax.fori_loop(0, 8, row_block, 0)


def product(left_ref, rows, high, low, out):
    def column_block(n, carry):
        lanes = pl.ds(pl.multiple_of(n * 256, 256), 256)
        ah, al = halves(left_ref[rows, :])
        bh = high[:, lanes]
        out[:, lanes] = dot(ah, bh) + dot(al, bh) + dot(ah, low[:, lanes])
        return carry

    lax.fori_loop(0, 4, column_block, 0)


def unweave(to_planes):
    row, col = iota((128, 128), 0), iota((128, 128), 1)
    if not to_planes:
        row, col = col, row
    source = jnp.where(row < 64, 2 * row, 2 * row - 127)
    return jnp.where(col == source, 1.0, 0.0).astype(BF16)


def fast_kernel(scale, trial, applied, extra, gt_ref, gx_ref, z_ref, ok_ref, t_ref, x_ref, gt, part, core_in, mid, x_in,
                ring, full, dcol, drow, left_a, left_b, right_a, right_b, right_c, one, two, three, four, t_send,
                t_recv, x_send, x_recv, s_send, s_recv, local_sem):
    g = lax.axis_index("ga")
    b = lax.axis_index("band")
    zl, x, c = g // 8, (g // 2) % 4, g % 2
    h, y = b // 4, b % 4
    partner = (1 - h) * 4 + y
    y_up, y_dn, y_far = (y + 1) % 4, (y + 3) % 4, (y + 2) % 4

    def band_at(hh, yy):
        return hh * 4 + yy

    def ga_at(zz, xx, cc):
        return zz * 8 + xx * 2 + cc

    def ring_at(d):
        z = (h * 4 + zl + d) % 8
        return (ga_at(z % 4, x, c), band_at(z // 4, y))

    sib = (ga_at(zl, x, 1 - c), b)
    xs = [(ga_at(zl, (x + d) % 4, c), b) for d in range(1, 4)]
    ys = [(g, band_at(h, (y + d) % 4)) for d in range(1, 4)]
    rings = [ring_at(d) for d in range(1, 8)]
    barrier = pltpu.get_barrier_semaphore()
    greet = [sib] + xs + ys + rings
    for device in greet:
        pl.semaphore_signal(barrier, inc=1, device_id=device, device_id_type=MESH)
    planes = unweave(True)
    t_ref[...] = dot(planes, trial[...].reshape(128, 1024)).astype(BF16)
    pl.semaphore_wait(barrier, len(greet))

    up, dn, over = (g, band_at(h, y_up)), (g, band_at(h, y_dn)), (g, partner)
    b_dn, b_up, b_far = band_at(h, y_dn), band_at(h, y_up), band_at(h, y_far)
    p_dn, p_up, p_far = band_at(1 - h, y_dn), band_at(1 - h, y_up), band_at(1 - h, y_far)

    class Gather:
        def __init__(self, own, slots, size, send, recv):
            def move(n, src, block, rows, device):
                return remote(src, slots.at[block, rows], send.at[n], recv.at[n], device)

            def relay(n, block, rows, device):
                return move(n, slots.at[block, rows], block, rows, device)

            step = size // 4
            piece = [pl.ds(n * step, step) for n in range(4)]
            whole, lo, hi = pl.ds(0, size), pl.ds(0, size // 2), pl.ds(size // 2, size // 2)
            self.cross = [move(n, own.at[piece[n]], b, piece[n], over) for n in range(4)]
            self.near = [move(4, own, b, whole, up), move(5, own, b, whole, dn)]
            self.far = [relay(6, b_dn, lo, up), relay(7, b_up, hi, dn)]
            self.to_up = [relay(8 + n, partner, piece[n], up) for n in range(4)]
            self.to_dn = [relay(12 + n, partner, piece[n], dn) for n in range(4)]
            self.last = [relay(16, p_dn, piece[0], up), relay(17, p_dn, piece[1], up)]
            self.last += [relay(18, p_up, piece[2], dn), relay(19, p_up, piece[3], dn)]

        def start_near(self):
            for copy in self.near:
                copy.start()

        def start_cross(self, first, count):
            for copy in self.cross[first : first + count]:
                copy.start()

        def pass_own(self):
            for n in range(2):
                self.near[n].wait_recv()
                self.far[n].start()

        def pass_cross(self, n):
            self.cross[n].wait_recv()
            self.to_up[n].start()
            self.to_dn[n].start()

        def pass_last(self, n):
            (self.to_up if n < 2 else self.to_dn)[n].wait_recv()
            self.last[n].start()

        def finish(self):
            for copy in self.far + self.to_up[2:] + self.to_dn[:2] + self.last:
                copy.wait_recv()

        def drain(self):
            for copy in self.cross + self.near + self.far + self.to_up + self.to_dn + self.last:
                copy.wait_send()

    tg = Gather(t_ref, gt, 128, t_send, t_recv)
    xg = Gather(x_ref, gx_ref, 256, x_send, x_recv)

    sign = jnp.where(iota((64, 128), 1) < 64, scale, -scale).astype(F32)

    def gram(k, block):
        u = lax.dot_general(x_ref[...], block, (((1,), (1,)), ((), ())), preferred_element_type=F32)
        part[1, k] = u[0:64] * sign + pltpu.roll(u[64:128], 64, 1) * scale
        part[0, k] = u[128:192] * sign + pltpu.roll(u[192:256], 64, 1) * scale

    tg.start_cross(0, 1)
    tg.start_near()
    tg.start_cross(1, 3)
    x_ref[0:128] = dot(planes, applied[...].reshape(128, 1024)).astype(BF16)
    margin = (trial[...].astype(F32) + extra[...].astype(F32)).astype(BF16)
    x_ref[128:256] = dot(planes, margin.reshape(128, 1024)).astype(BF16)
    own_x = pltpu.make_async_copy(x_ref, gx_ref.at[b], local_sem.at[1])
    own_x.start()
    gt[b] = t_ref[...]
    gram(b, t_ref[...])
    tg.pass_cross(0)
    tg.pass_own()
    tg.pass_cross(1)
    tg.pass_last(0)
    tg.pass_cross(2)
    tg.pass_last(1)
    tg.pass_cross(3)
    xg.start_cross(0, 2)
    gram(b_dn, gt[b_dn])
    gram(b_up, gt[b_up])
    gram(partner, gt[partner])
    tg.pass_last(2)
    tg.pass_last(3)
    tg.finish()
    xg.start_near()
    for k in (b_far, p_dn, p_up, p_far):
        gram(k, gt[k])

    blk = c * 4 + x
    lane64 = iota((64, 128), 1) < 64
    eye = iota((64, 128), 0) == iota((64, 128), 1)
    eye_im = iota((64, 128), 0) + 64 == iota((64, 128), 1)

    def rounded(value):
        return value.astype(BF16).astype(F32)

    def core_moves(m):
        return [remote(part.at[m, pl.ds((1 - c) * 4, 4)], core_in.at[m], s_send.at[m, 0], s_recv.at[m, 0], sib)]

    def core_add(m):
        mid[m] = part[m, pl.ds(c * 4, 4)] + core_in[m]

    def x_moves(m):
        return [
            remote(mid.at[m, (x + d) % 4], x_in.at[m, d - 1], s_send.at[m, d], s_recv.at[m, d], xs[d - 1])
            for d in range(1, 4)
        ]

    def x_add(m):
        value = mid[m, x] + x_in[m, 0] + x_in[m, 1] + x_in[m, 2]
        turned = pltpu.roll(value, 64, 1)
        ring[m, h, zl] = jnp.where(eye_im & (blk == b), turned - rounded(turned), value).astype(BF16)

    def spread(m, view, base, devices):
        return [
            remote(view, view, s_send.at[m, base + n], s_recv.at[m, base + n], device)
            for n, device in enumerate(devices)
        ]

    def ring_add(m):
        for hh in range(2):
            value = ring[m, hh, 0].astype(F32)
            for n in range(1, 4):
                value = value + ring[m, hh, n].astype(F32)
            exact = value + pltpu.roll(value, 64, 1)
            mine = blk == hh * 4 + y
            value = jnp.where(eye & mine, exact, jnp.where(eye_im & mine, exact - rounded(exact), value))
            full[m, blk, hh, y] = value.astype(BF16)

    stages = [
        (core_moves, core_add),
        (x_moves, x_add),
        (lambda m: spread(m, ring.at[m, h, zl], 4, rings), ring_add),
        (lambda m: spread(m, full.at[m, blk, :, y], 11, ys), None),
        (lambda m: spread(m, full.at[m, blk], 14, xs), None),
        (lambda m: spread(m, full.at[m, pl.ds(c * 4, 4)], 17, [sib]), None),
    ]
    flight = {}

    def launch(n, m):
        flight[n, m] = stages[n][0](m)
        for move in flight[n, m]:
            move.start()

    def land(n, m):
        for move in flight[n, m]:
            move.wait()
        if stages[n][1] is not None:
            stages[n][1](m)

    def turn(n):
        land(n, 0)
        launch(n + 1, 0)
        land(n, 1)
        launch(n + 1, 1)

    launch(0, 0)
    out_t = pltpu.make_async_copy(gt, gt_ref, local_sem.at[0])
    out_t.start()
    land(0, 0)
    launch(1, 0)
    launch(0, 1)
    land(1, 0)
    launch(2, 0)
    land(0, 1)
    launch(1, 1)
    land(2, 0)
    launch(3, 0)
    land(1, 1)
    launch(2, 1)
    land(3, 0)
    launch(4, 0)
    land(2, 1)
    launch(3, 1)
    xg.start_cross(2, 2)
    xg.pass_own()
    xg.pass_cross(0)
    xg.pass_cross(1)
    land(4, 0)
    launch(5, 0)
    land(3, 1)
    launch(4, 1)
    land(5, 0)

    def tile(m, n, k, count):
        block = full[m, n, k // 4, pl.ds(k % 4, count)]
        return block.astype(F32).reshape(64 * count, 128)

    def scales(k, carry):
        rows = pl.ds(pl.multiple_of(k * 64, 64), 64)
        block = tile(0, k, k, 1)
        diagonal = jnp.where(eye, block + pltpu.roll(block, 64, 1), 0.0)
        dcol[rows, :] = jnp.broadcast_to(lax.rsqrt(jnp.sum(diagonal, axis=1, keepdims=True)), (64, 128))
        across = jnp.sum(diagonal, axis=0, keepdims=True)
        across = lax.rsqrt(across + pltpu.roll(across, 64, 1))
        drow[:, pl.ds(pl.multiple_of(k * 128, 128), 128)] = jnp.broadcast_to(across, (8, 128))
        return carry

    lax.fori_loop(0, 8, scales, 0, unroll=True)

    def scaled_rows(m, k, factor, out, left_out, right_out):
        rows = pl.ds(pl.multiple_of(k * 64, 64), 64)
        top, bottom = pl.ds(pl.multiple_of(k * 128, 128), 64), pl.ds(pl.multiple_of(k * 128 + 64, 64), 64)
        left = dcol[rows, :] * (0.5 * factor)
        for n in range(0, 8, 2):
            turned = tile(m, k, n, 2).T
            re, im = turned[0:64], -turned[64:128]
            back = (
                jnp.where(lane64, re, pltpu.roll(im, 64, 1)),
                jnp.where(lane64, pltpu.roll(re, 64, 1), im),
            )
            for i in range(2):
                lanes = pl.ds(128 * (n + i), 128)
                right = drow[0:1, lanes]
                block = tile(m, n + i, k, 1)
                value = (block + back[i]) * left * right
                if m == 0:
                    value = jnp.where((eye | eye_im) & (k == n + i), 0.0, value)
                    left_out[rows, lanes] = value.astype(BF16)
                else:
                    exact = (block + pltpu.roll(block, 64, 1)) * 2.0 * left * right
                    value = jnp.where(eye & (k == n + i), exact, value)
                    value = jnp.where(eye_im & (k == n + i), 0.0, value)
                out[rows, lanes] = value
                right_out[top, lanes] = value.astype(BF16)
                right_out[bottom, lanes] = times_i(value).astype(BF16)

    def put_right(right, lanes, value):
        turned = times_i(value)
        for k in range(8):
            rows = slice(64 * k, 64 * k + 64)
            right[pl.ds(128 * k, 64), lanes] = value[rows].astype(BF16)
            right[pl.ds(128 * k + 64, 64), lanes] = turned[rows].astype(BF16)

    def by_columns(body, init=0):
        def column_block(n, carry):
            return body(n, pl.ds(pl.multiple_of(n * 256, 256), 256), carry)

        return lax.fori_loop(0, 4, column_block, init, unroll=True)

    def column_sum(value):
        return jnp.sum(value, axis=0, keepdims=True)

    zero_row = jnp.zeros((1, 256), F32)

    def margin_rows(k, carry):
        scaled_rows(0, k, -1.0, one, left_a, right_a)
        return carry

    lax.fori_loop(0, 8, margin_rows, 0)
    xg.pass_cross(2)
    land(4, 1)
    launch(5, 1)

    def second_power(n, lanes, carry):
        value = dot(left_a[...], right_a[:, lanes])
        two[:, lanes] = value
        put_right(right_b, lanes, value + one[:, lanes])
        return carry

    by_columns(second_power)
    xg.pass_cross(3)
    xg.pass_last(0)
    land(5, 1)

    def third_power(n, lanes, carry):
        value = dot(left_a[...], right_b[:, lanes])
        cube = value - two[:, lanes]
        left_b[:, lanes] = cube.astype(BF16)
        one[:, lanes] = one[:, lanes] + value
        scaled_rows(1, 2 * n, 1.0, four, None, right_c)
        scaled_rows(1, 2 * n + 1, 1.0, four, None, right_c)
        return carry + column_sum(cube * cube)

    cube_norm = by_columns(third_power, zero_row)
    xg.pass_last(1)

    def series(n, lanes, carry):
        value = one[:, lanes] + dot(left_b[...], right_b[:, lanes])
        two[:, lanes] = value
        left_a[:, lanes] = value.astype(BF16)
        put_right(right_a, lanes, value)
        return carry

    by_columns(series)
    xg.pass_last(2)
    xg.pass_last(3)

    def first_product(n, lanes, carry):
        value = four[:, lanes] + dot(left_a[...], right_c[:, lanes])
        one[:, lanes] = value
        left_b[:, lanes] = value.astype(BF16)
        return carry

    by_columns(first_product)

    def second_product(n, lanes, carry):
        value = one[:, lanes] + dot(left_b[...], right_a[:, lanes])
        three[:, lanes] = value
        put_right(right_b, lanes, value)
        return (carry[0] + column_sum(value * four[:, lanes]), carry[1] + column_sum(value * one[:, lanes]))

    sums = by_columns(second_product, (zero_row, zero_row))
    trace_qh = jnp.sum(sums[0], keepdims=True)
    trace_pq = jnp.sum(sums[1], keepdims=True)
    rs = lax.rsqrt(jnp.maximum(trace_qh, 0.0) * (1.0 / 512) + 1e-6)
    own = pl.ds(pl.multiple_of(b * 64, 64), 64)
    own_lanes = pl.ds(pl.multiple_of(b * 128, 128), 128)
    product = dot(left_b[own, :], right_b[...])
    four[own, :] = two[own, :] - three[own, :] * rs + product * (0.25 * rs * rs)
    four[own, own_lanes] = four[own, own_lanes] + jnp.where(eye, 1.0, 0.0)
    left = jnp.concatenate([dcol[own, :]] * 8, axis=1)
    z_ref[...] = rotation_weights(rounded(four[own, :] * left * drow[0:1, :]))

    def trace_of(ref):
        total = jnp.zeros((64, 128), F32)
        for k in range(8):
            total = total + jnp.where(eye, ref[pl.ds(k * 64, 64), pl.ds(k * 128, 128)], 0.0)
        return jnp.sum(total, keepdims=True)

    trace_w = 512.0 + trace_of(two)
    trace_z = trace_w - trace_of(three) * rs + trace_pq * (0.25 * rs * rs)
    small = jnp.sum(cube_norm, keepdims=True) < 0.0225
    ok = small & (trace_z > 0.6 * trace_w)
    ok_ref[...] = jnp.broadcast_to(jnp.where(ok, 1, 0).astype(jnp.int32), (8, 128))

    xg.finish()
    tg.drain()
    xg.drain()
    own_x.wait()
    out_t.wait()


def fast_filter(trial, applied, extra, scale):
    vmem = pl.BlockSpec(memory_space=pltpu.VMEM)
    anywhere = pl.BlockSpec(memory_space=pl.ANY)
    sem = pltpu.SemaphoreType.DMA
    square = pltpu.VMEM((512, 1024), F32)
    left = pltpu.VMEM((512, 1024), BF16)
    right = pltpu.VMEM((1024, 1024), BF16)
    return pl.pallas_call(
        functools.partial(fast_kernel, scale),
        out_shape=(
            jax.ShapeDtypeStruct((8, 128, 1024), BF16),
            jax.ShapeDtypeStruct((8, 256, 1024), BF16),
            jax.ShapeDtypeStruct((128, 1024), BF16),
            jax.ShapeDtypeStruct((8, 128), jnp.int32),
        ),
        in_specs=[vmem] * 3,
        out_specs=(anywhere, anywhere, vmem, vmem),
        scratch_shapes=[
            pltpu.VMEM((128, 1024), BF16),
            pltpu.VMEM((256, 1024), BF16),
            pltpu.VMEM((8, 128, 1024), BF16),
            pltpu.VMEM((2, 8, 64, 128), F32),
            pltpu.VMEM((2, 4, 64, 128), F32),
            pltpu.VMEM((2, 4, 64, 128), F32),
            pltpu.VMEM((2, 3, 64, 128), F32),
            pltpu.VMEM((2, 2, 4, 64, 128), BF16),
            pltpu.VMEM((2, 8, 2, 4, 64, 128), BF16),
            pltpu.VMEM((512, 128), F32),
            pltpu.VMEM((8, 1024), F32),
            left,
            left,
            right,
            right,
            right,
            square,
            square,
            square,
            square,
            sem((20,)),
            sem((20,)),
            sem((20,)),
            sem((20,)),
            sem((2, 18)),
            sem((2, 18)),
            sem((2,)),
        ],
        compiler_params=pltpu.CompilerParams(
            collective_id=1, has_side_effects=True, vmem_limit_bytes=48 * 2**20
        ),
    )(trial, applied, extra)


def rotation_weights(z):
    turned = times_i(z)
    re_part = jnp.where(iota((64, 1024), 1) % 128 < 64, z, -z)
    im_part = jnp.where(iota((64, 1024), 1) % 128 < 64, -turned, turned)
    both = jnp.concatenate([re_part, im_part], axis=0).astype(BF16)
    return dot(unweave(False), both).astype(BF16)


def turn_blocks(weights, gt, gx, outs):
    width = gt.shape[2]
    sources = (gt[...], gx[:, 0:128, :], gx[:, 128:256, :])
    for out, source in zip(outs, sources):
        value = dot(weights, source.reshape(1024, width)).astype(BF16)
        out[...] = value.reshape(64, 2, width)


def fast_rotate_kernel(z_ref, gt, gx, *outs):
    turn_blocks(z_ref[...], gt, gx, outs)


def fast_rotate(z, gt, gx):
    width = 512
    return pl.pallas_call(
        fast_rotate_kernel,
        grid=(1024 // width,),
        out_shape=(jax.ShapeDtypeStruct((64, 2, 1024), BF16),) * 3,
        in_specs=[
            pl.BlockSpec((128, 1024), lambda n: (0, 0)),
            pl.BlockSpec((8, 128, width), lambda n: (0, 0, n)),
            pl.BlockSpec((8, 256, width), lambda n: (0, 0, n)),
        ],
        out_specs=(pl.BlockSpec((64, 2, width), lambda n: (0, 0, n)),) * 3,
        compiler_params=pltpu.CompilerParams(vmem_limit_bytes=48 * 2**20),
    )(z, gt, gx)


def rotate_kernel(full, gt, gx, o_ref, o_next, o_last, w, ham, p, q, pq, high, low):
    b = lax.axis_index("band")
    own = pl.ds(pl.multiple_of(b * 64, 64), 64)
    hermitian_part(full, 0, w)
    hermitian_part(full, 1, ham)
    invert(w)
    expand(ham, high, low)
    product(w, pl.ds(0, 512), high, low, p)
    expand(w, high, low)
    product(p, pl.ds(0, 512), high, low, q)
    total = jnp.sum(q[...] * ham[...], keepdims=True)
    rs = lax.rsqrt(jnp.maximum(total, 0.0) * (1.0 / 512) + 1e-6)
    expand(q, high, low)
    product(p, own, high, low, pq)
    z = w[own, :] - q[own, :] * rs + pq[...] * (0.25 * rs * rs)
    turn_blocks(rotation_weights(z.astype(BF16).astype(F32)), gt, gx, (o_ref, o_next, o_last))


def rotate(full, gt, gx):
    vmem = pl.BlockSpec(memory_space=pltpu.VMEM)
    return pl.pallas_call(
        rotate_kernel,
        out_shape=(jax.ShapeDtypeStruct((64, 2, 1024), BF16),) * 3,
        in_specs=[vmem] * 3,
        out_specs=(vmem,) * 3,
        scratch_shapes=[
            pltpu.VMEM((512, 1024), F32),
            pltpu.VMEM((512, 1024), F32),
            pltpu.VMEM((512, 1024), F32),
            pltpu.VMEM((512, 1024), F32),
            pltpu.VMEM((64, 1024), F32),
            pltpu.VMEM((1024, 1024), BF16),
            pltpu.VMEM((1024, 1024), BF16),
        ],
        compiler_params=pltpu.CompilerParams(vmem_limit_bytes=48 * 2**20),
    )(full, gt, gx)


def local(trial, applied, extra):
    rows, _, length = trial.shape
    scale = 1.0 / (length * lax.axis_size("ga"))
    gt, gx, z, ok = fast_filter(trial, applied, extra, scale)

    def planes(block):
        return jnp.swapaxes(block, 0, 1).reshape(2 * rows, length)

    def direct():
        margin = (trial.astype(F32) + extra.astype(F32)).astype(BF16)
        rest = jnp.concatenate([planes(applied), planes(margin)], axis=0)
        blocks, others, full = exchange(planes(trial), rest, scale)
        return tuple(rotate(full.reshape(2, 8, 512, 128), blocks, others))

    return lax.cond(ok[0, 0] > 0, lambda: tuple(fast_rotate(z, gt, gx)), direct)


def solution(mesh):
    spec = P("band", None, "ga")
    return jax.shard_map(local, mesh=mesh, in_specs=(spec,) * 3, out_specs=(spec,) * 3, check_vma=False)
```
